32 devices in a mesh: seq: 8 (over z, y), chan: 4 (over x, core).
Axes of the slice: x: 2, y: 2, z: 4, core: 2. Of those that a mesh axis runs over, the one named last changes fastest.
Arguments:
- stream: bfloat16 [2048, 4096], P('seq', 'chan'), may hold values from -60 to 60
- norm_gain: float32 [4096], P('chan'), may hold values from 0.1 to 1.9
- gate_query: bfloat16 [2048, 4096], P('seq', 'chan'), may hold values from -6 to 6
- gate_key: bfloat16 [2048, 4096], P('seq', 'chan'), may hold values from -6 to 6
- gate_out: bfloat16 [2048, 4096], P('seq', 'chan'), may hold values from -6 to 6
- cotangent: bfloat16 [2048, 4096], P('seq', 'chan'), may hold values from -6 to 6
- medium_filter: float32 [128, 4096], P(None, 'chan'), may hold values from -0.53033009 to 0.53033009
- long_residue: float32 [4096], P('chan'), may hold values from 0.5 to 1.5
- long_rate: float32 [4096], P('chan'), may hold values from 0.000146484375 to 0.0333333333
Outputs:
- grad_query: bfloat16 [2048, 4096], P('seq', 'chan')
- grad_stream: bfloat16 [2048, 4096], P('seq', 'chan')
- grad_filter: float32 [128, 4096], P(None, 'chan')
- grad_residue: float32 [4096], P('chan')
The draws below stay inside these ranges and needn't reach their ends.
All inputs are finite; a program needn't handle non-finite values.
Results may differ from the reference program's by a relative error of at most 0.008.
Values sent between devices are 32-bit elements; how exact they have to be, the bound alone decides.
A program may use at most 64 MiB of HBM per device.

```python
import math
import jax
import jax.numpy as jnp
from jax import lax

CHANNELS = 4096
FILTER_TAPS = 128
TOKENS = 2048


def region_field(key, lowest, highest):
    group_count = 16
    segment_rows = 16
    field = jnp.exp(jax.random.uniform(key, (TOKENS // segment_rows, 1, group_count, 1), jnp.float32, math.log(lowest), math.log(highest)))
    field = jnp.broadcast_to(field, (TOKENS // segment_rows, segment_rows, group_count, CHANNELS // group_count))
    return field.reshape(TOKENS, CHANNELS)


def make_stream(key):
    first_key = jax.random.fold_in(jax.random.fold_in(key, 101), 0)
    second_key = jax.random.fold_in(jax.random.fold_in(key, 101), 1)
    third_key = jax.random.fold_in(jax.random.fold_in(key, 101), 2)
    fifth_key = jax.random.fold_in(jax.random.fold_in(key, 101), 4)
    base = jnp.clip(jax.random.normal(first_key, (TOKENS, CHANNELS), jnp.float32), -4.0, 4.0)
    row_scale = jnp.exp(jax.random.uniform(second_key, (TOKENS, 1), jnp.float32, math.log(0.3), math.log(3.0)))
    jitter = jnp.exp(jax.random.uniform(third_key, (1, CHANNELS), jnp.float32, -0.3, 0.3))
    region = region_field(fifth_key, 0.3, 3.0)
    return base * row_scale * region * jitter


def draw_stream(key, part):
    return make_stream(key).astype(jnp.bfloat16)


def draw_gate_key(key, part):
    own_key = jax.random.fold_in(key, 202)
    magnitude = jnp.clip(jax.random.normal(own_key, (TOKENS, CHANNELS), jnp.float32), -6.0, 6.0)
    return magnitude.astype(jnp.bfloat16)


def positive_or_normal(key):
    values = jnp.clip(jax.random.normal(key, (TOKENS, CHANNELS), jnp.float32), -6.0, 6.0)
    return values


def draw_gate_query(key, part):
    return positive_or_normal(jax.random.fold_in(key, 303)).astype(jnp.bfloat16)


def draw_gate_out(key, part):
    return positive_or_normal(jax.random.fold_in(key, 404)).astype(jnp.bfloat16)


def draw_cotangent(key, part):
    noise_key = jax.random.fold_in(jax.random.fold_in(key, 505), 1)
    noise = jax.random.normal(noise_key, (TOKENS, CHANNELS), jnp.float32)
    values = jnp.clip(noise, -6.0, 6.0)
    return values.astype(jnp.bfloat16)


def draw_medium_filter(key, part):
    own_key = jax.random.fold_in(key, 606)
    spread = FILTER_TAPS ** (-0.5)
    values = jax.random.normal(own_key, (FILTER_TAPS, CHANNELS), jnp.float32)
    values = jnp.clip(values, -6.0, 6.0)
    return (values * spread).astype(jnp.float32)


def draw_long_rate(key, part):
    first_key, second_key = jax.random.split(key, 2)
    slow_flag = jax.random.randint(first_key, (CHANNELS,), 0, 2)
    fraction = jax.random.uniform(second_key, (CHANNELS,), jnp.float32)
    slow_rate = jnp.exp(math.log(0.3 / TOKENS) + fraction * math.log(2.0 / 0.3))
    fast_rate = jnp.exp(math.log(1.0 / 50.0) + fraction * math.log(50.0 / 30.0))
    return jnp.where(slow_flag == 1, slow_rate, fast_rate).astype(jnp.float32)


def block_levels(key, dims, shards, smallest, top_value):
    def one(position, parts):
        draws = jax.random.uniform(jax.random.fold_in(jax.random.fold_in(key, 6), position), (parts,), jnp.float32, smallest / len(shards), top_value / len(shards))
        return jnp.repeat(jnp.exp(draws), dims[position] // parts).reshape((-1,) + (1,) * (len(dims) - position - 1))

    gain = one(*shards[0])
    for cut in shards[1:]:
        gain = gain * one(*cut)
    return gain


def setup_inputs(seed: int = 0) -> dict:
    splits = jax.random.split(jax.random.key(seed), 10)
    return {
        "stream": draw_stream(jax.random.fold_in(splits[9], 71), 0),
        "norm_gain": jnp.clip(1.0 + 0.18 * jax.random.normal(splits[1], (CHANNELS,), jnp.float32), 0.1, 1.9),
        "gate_query": draw_gate_query(jax.random.fold_in(splits[9], 71), 0),
        "gate_key": draw_gate_key(jax.random.fold_in(splits[9], 71), 0),
        "gate_out": draw_gate_out(jax.random.fold_in(splits[9], 71), 0),
        "cotangent": draw_cotangent(jax.random.fold_in(splits[9], 71), 0),
        "medium_filter": draw_medium_filter(jax.random.fold_in(splits[9], 71), 0),
        "long_residue": jnp.clip(0.5 + 1.0 * jax.random.uniform(splits[7], (CHANNELS,), jnp.float32) ** block_levels(splits[7], (CHANNELS,), ((0, 4),), -0.2, 0.2), 0.5, 1.5),
        "long_rate": draw_long_rate(jax.random.fold_in(splits[9], 71), 0),
    }


EPSILON = 1e-05

def decayed_reverse(source, decay_row):

    def advance(carry, row_value):
        carry = decay_row * carry + row_value
        return (carry, carry)
    initial = jnp.zeros(source.shape[1:], jnp.float32)
    return lax.scan(advance, initial, source, reverse=True)[1]

def channel_block(operands):
    normed_block, query_block, key_block, outgate_block, cotan_block, filter_block, residue_block, rate_block = operands
    rim_width = FILTER_TAPS - 1
    block_width = normed_block.shape[1]
    product = key_block.astype(jnp.float32) * normed_block
    padded = jnp.concatenate([jnp.zeros((rim_width, block_width), jnp.float32), product], axis=0)

    def forward_tap(tap_index, running_sum):
        start = (rim_width - tap_index).astype(jnp.int32)
        shifted = lax.dynamic_slice_in_dim(padded, start, TOKENS, 0)
        return running_sum + filter_block[tap_index] * shifted
    mixed_rows = lax.fori_loop(0, FILTER_TAPS, forward_tap, jnp.zeros((TOKENS, block_width), jnp.float32))
    stored = (query_block.astype(jnp.float32) * mixed_rows).astype(jnp.bfloat16)
    normalizer = jnp.sqrt(-jnp.expm1(-2.0 * rate_block))
    grad_source = outgate_block.astype(jnp.float32) * cotan_block.astype(jnp.float32)
    reverse_state = decayed_reverse(grad_source, jnp.exp(-rate_block))
    grad_stored = residue_block * normalizer * reverse_state
    grad_query = (mixed_rows * grad_stored).astype(jnp.bfloat16)
    grad_mixed = query_block.astype(jnp.float32) * grad_stored
    trailing = jnp.concatenate([grad_mixed, jnp.zeros((rim_width, block_width), jnp.float32)], axis=0)

    def backward_tap(tap_index, running_sum):
        shifted = lax.dynamic_slice_in_dim(trailing, tap_index.astype(jnp.int32), TOKENS, 0)
        return running_sum + filter_block[tap_index] * shifted
    grad_product = lax.fori_loop(0, FILTER_TAPS, backward_tap, jnp.zeros((TOKENS, block_width), jnp.float32))
    grad_normed = key_block.astype(jnp.float32) * grad_product

    def filter_tap(tap_index):
        start = (rim_width - tap_index).astype(jnp.int32)
        shifted = lax.dynamic_slice_in_dim(padded, start, TOKENS, 0)
        return lax.optimization_barrier(jnp.sum(grad_mixed * shifted, axis=0))
    grad_scale = TOKENS ** (-0.5)
    grad_filter = lax.map(filter_tap, jnp.arange(FILTER_TAPS, dtype=jnp.int32)) * grad_scale
    grad_residue = normalizer * lax.optimization_barrier(jnp.sum(stored.astype(jnp.float32) * reverse_state, axis=0)) * grad_scale
    return (grad_query, grad_normed, grad_filter, grad_residue)

def reference(stream, norm_gain, gate_query, gate_key, gate_out, cotangent, medium_filter, long_residue, long_rate):
    inputs = stream.astype(jnp.float32)
    inv_rms = lax.rsqrt(lax.optimization_barrier(jnp.mean(inputs * inputs, axis=1, keepdims=True)) + EPSILON)
    normed = inputs * inv_rms * norm_gain
    block_width = math.gcd(CHANNELS, 256)
    block_count = CHANNELS // block_width

    def split_cols(matrix):
        return jnp.moveaxis(matrix.reshape(matrix.shape[0], block_count, block_width), 1, 0)

    def join_cols(stack):
        return jnp.moveaxis(stack, 0, 1).reshape(stack.shape[1], CHANNELS)
    results = lax.map(channel_block, (split_cols(normed), split_cols(gate_query), split_cols(gate_key), split_cols(gate_out), split_cols(cotangent), split_cols(medium_filter), long_residue.reshape(block_count, block_width), long_rate.reshape(block_count, block_width)))
    grad_query = join_cols(results[0])
    grad_normed = join_cols(results[1])
    grad_filter = join_cols(results[2])
    grad_residue = results[3].reshape(CHANNELS)
    weighted = norm_gain * grad_normed
    row_dots = lax.optimization_barrier(jnp.mean(weighted * inputs, axis=1, keepdims=True))
    grad_stream = (inv_rms * (weighted - inputs * inv_rms * inv_rms * row_dots)).astype(jnp.bfloat16)
    return (grad_query, grad_stream, grad_filter, grad_residue)
```

```python
import functools

import jax
import jax.numpy as jnp
import ml_dtypes
import numpy as np
from jax import lax
from jax.experimental import pallas as pl
from jax.experimental.pallas import tpu as pltpu
from jax.sharding import PartitionSpec as P

EPSILON = 1e-05
F32 = jnp.float32
BF16 = jnp.bfloat16
MESH = pl.DeviceIdType.MESH
WIDE = 256


def split_np(matrix):
    high = matrix.astype(ml_dtypes.bfloat16)
    low = (matrix - high.astype(np.float64)).astype(ml_dtypes.bfloat16)
    return np.stack([high, low])


def transforms(rows, taps):
    length = rows + taps
    freqs = np.arange(length // 2)[:, None] * 2 + 1
    turns = (freqs * np.arange(length)[None, :]) % (2 * length)
    angle = np.pi * turns / length
    forward = np.concatenate([np.cos(angle), -np.sin(angle)], axis=0)
    inverse = forward.T * (2.0 / length)
    lags = inverse[taps - np.arange(taps)]
    return split_np(forward), split_np(inverse), split_np(lags)


def halves(value):
    high = value.astype(BF16)
    low = (value - high.astype(F32)).astype(BF16)
    return high, low


def product3(mat_ref, rows, cols, value):
    high, low = halves(value)
    mat_high = mat_ref[0, rows, cols]
    mat_low = mat_ref[1, rows, cols]
    total = jnp.dot(mat_high, high, preferred_element_type=F32)
    total += jnp.dot(mat_low, high, preferred_element_type=F32)
    return total + jnp.dot(mat_high, low, preferred_element_type=F32)


def kernel(
    n,
    m,
    stream,
    gain,
    query,
    key,
    gate_out,
    cotangent,
    taps_ref,
    residue,
    rate,
    fwd,
    inv,
    lag,
    out_query,
    out_stream,
    out_filter,
    out_residue,
    raw,
    entering,
    rev,
    gm,
    raw_halo,
    gm_halo,
    inv_col,
    row_send,
    row_recv,
    inv_halo,
    carry_send,
    carry_recv,
    fh,
    xh,
    gh,
    gf,
    rs_recv,
    ag,
    res_all,
    weighted,
    halo_sem,
    row_sem,
    carry_sem,
    rs_sem,
    ag_sem,
    res_sem,
):
    s, c = lax.axis_index("seq"), lax.axis_index("chan")
    R, C = stream.shape
    K = taps_ref.shape[0]
    N = R + K
    H = N // 2
    chunk = gf.shape[1]
    channel_total = C * m
    token_total = R * n

    barrier = pltpu.get_barrier_semaphore()

    def greet(d, _):
        pl.semaphore_signal(barrier, inc=1, device_id=(lax.rem(s + d, n), c), device_id_type=MESH)
        return 0

    lax.fori_loop(1, n, greet, 0)
    for d in range(1, m):
        pl.semaphore_signal(barrier, inc=1, device_id=(s, lax.rem(c + d, m)), device_id_type=MESH)

    def tiles(width, step, init=0):
        def run(i, carry):
            return step(pl.ds(pl.multiple_of(i * width, width), width), carry)

        return lax.fori_loop(0, C // width, run, init)

    def lanes(value):
        return sum(value[:, i * 128 : (i + 1) * 128] for i in range(value.shape[1] // 128))

    def wide(col):
        return jnp.concatenate([col] * (WIDE // 128), axis=1)

    def to_row(acc):
        return jnp.broadcast_to(jnp.sum(acc.T, axis=0, keepdims=True), (8, R))

    def to_col(row):
        return jnp.broadcast_to(row[0:1, :], (128, R)).T

    def copy(src, dst, sems, index, target):
        return pltpu.make_async_remote_copy(
            src_ref=src,
            dst_ref=dst,
            send_sem=sems.at[0, index],
            recv_sem=sems.at[1, index],
            device_id=target,
            device_id_type=MESH,
        )

    def first(cols, acc):
        x = stream[:, cols].astype(F32)
        raw[:, cols] = key[:, cols].astype(F32) * x * gain[:, cols]
        return acc + lanes(x * x)

    squares = to_row(tiles(WIDE, first, jnp.zeros((R, 128), F32)))
    row_send[0] = squares

    pl.semaphore_wait(barrier, n - 1 + m - 1)

    def row_copy(kind, d):
        return copy(
            row_send.at[kind],
            row_recv.at[kind, d - 1],
            row_sem,
            kind * (m - 1) + d - 1,
            (s, lax.rem(c + d, m)),
        )

    after = (lax.rem(s + 1, n), c)
    before = (lax.rem(s + n - 1, n), c)
    halo_copy = copy(raw.at[pl.ds(R - K, K), :], raw_halo, halo_sem, 0, after)
    inv_copy = copy(row_send.at[2], inv_halo, halo_sem, 1, after)
    gm_copy = copy(gm.at[pl.ds(0, K), :], gm_halo, halo_sem, 2, before)

    for d in range(1, m):
        row_copy(0, d).start()

    @pl.when(s < n - 1)
    def _():
        halo_copy.start()

    def recur(cols, _):
        value = gate_out[:, cols].astype(F32) * cotangent[:, cols].astype(F32)
        slow = rate[:, cols]
        row = lax.broadcasted_iota(jnp.int32, value.shape, 0)
        k = 1
        while k < R:
            factor = jnp.exp(-slow * k)
            if k < 8:
                moved = jnp.where(row < R - k, pltpu.roll(value, R - k, 0), 0.0)
            else:
                moved = jnp.concatenate([value[k:], jnp.zeros((k, value.shape[1]), F32)], axis=0)
            value = value + factor * moved
            k *= 2
        rev[:, cols] = value
        carry_send[:, cols] = value[0:1]
        return 0

    tiles(128, recur)

    def carry_copy(d):
        return copy(
            carry_send, carry_recv.at[d - 1], carry_sem, d - 1, (lax.rem(s + n - d, n), c)
        )

    def start_carry(d, _):
        carry_copy(d).start()
        return 0

    lax.fori_loop(1, s + 1, start_carry, 0)

    def tap_spectrum(cols, _):
        fh[:, cols] = product3(fwd, slice(None), slice(0, K), taps_ref[:, cols])
        return 0

    tiles(WIDE, tap_spectrum)

    total = squares
    for d in range(1, m):
        row_copy(0, d).wait_recv()
        total = total + row_recv[0, d - 1]
    inv_row = lax.rsqrt(total / channel_total + EPSILON)
    row_send[2] = inv_row
    inv_col[...] = to_col(inv_row)

    @pl.when(s < n - 1)
    def _():
        inv_copy.start()

    def local_spectrum(cols, _):
        value = raw[:, cols] * wide(inv_col[...])
        xh[:, cols] = product3(fwd, slice(None), slice(K, N), value)
        return 0

    tiles(WIDE, local_spectrum)

    def wait_carry(d, _):
        carry_copy(d).wait_recv()
        return 0

    lax.fori_loop(1, n - s, wait_carry, 0)
    block_decay = jnp.exp(-rate[...] * R)

    def horner(i, later):
        return block_decay * later + carry_recv[n - 2 - s - i]

    later_state = lax.fori_loop(0, n - 1 - s, horner, jnp.zeros((1, C), F32))
    entering[...] = later_state

    def norm_factor(slow):
        z = 2.0 * slow
        poly = 1.0 - z / 6.0
        for k in (5.0, 4.0, 3.0, 2.0):
            poly = 1.0 - z / k * poly
        return jnp.sqrt(z * poly)

    def state(cols, _):
        slow = rate[:, cols]
        position = lax.broadcasted_iota(jnp.int32, (R, WIDE), 0).astype(F32)
        value = rev[:, cols] + jnp.exp(-slow * (R - position)) * entering[:, cols]
        rev[:, cols] = value
        gm[:, cols] = query[:, cols].astype(F32) * (residue[:, cols] * norm_factor(slow) * value)
        return 0

    tiles(WIDE, state)

    @pl.when(s > 0)
    def _():
        gm_copy.start()

    def grad_spectrum(cols, _):
        gh[:, cols] = product3(fwd, slice(None), slice(0, R), gm[:, cols])
        return 0

    tiles(WIDE, grad_spectrum)

    @pl.when(s > 0)
    def _():
        inv_copy.wait_recv()
        halo_col = to_col(inv_halo[...])[R - K :]
        halo_copy.wait_recv()

        def halo_spectrum(cols, _):
            value = raw_halo[:, cols] * wide(halo_col)
            xh[:, cols] = xh[:, cols] + product3(fwd, slice(None), slice(0, K), value)
            return 0

        tiles(WIDE, halo_spectrum)

    def filter_grad(cols, _):
        xr, xi = xh[:H, cols], xh[H:, cols]
        gr, gi = gh[:H, cols], gh[H:, cols]
        spectrum = jnp.concatenate([gr * xr + gi * xi, gr * xi - gi * xr], axis=0)
        value = product3(lag, slice(None), slice(None), spectrum)
        for i in range(n):
            gf[i, :, cols] = value[i * chunk : (i + 1) * chunk]
        return 0

    tiles(WIDE, filter_grad)

    def rs_copy(d):
        owner = lax.rem(s + d, n)
        return copy(gf.at[owner], rs_recv.at[d - 1], rs_sem, d - 1, (owner, c))

    def start_rs(d, _):
        rs_copy(d).start()
        return 0

    lax.fori_loop(1, n, start_rs, 0)

    def forward(cols, _):
        xr, xi = xh[:H, cols], xh[H:, cols]
        fr, fi = fh[:H, cols], fh[H:, cols]
        spectrum = jnp.concatenate([fr * xr - fi * xi, fr * xi + fi * xr], axis=0)
        mixed = product3(inv, slice(K, N), slice(None), spectrum)
        factor = norm_factor(rate[:, cols])
        states = rev[:, cols]
        out_query[:, cols] = (mixed * (residue[:, cols] * factor * states)).astype(BF16)
        stored = (query[:, cols].astype(F32) * mixed).astype(BF16).astype(F32)
        res_all[s, :, cols] = factor * jnp.sum(stored * states, axis=0, keepdims=True)
        return 0

    tiles(WIDE, forward)

    def res_copy(d):
        return copy(res_all.at[s], res_all.at[s], res_sem, d - 1, (lax.rem(s + d, n), c))

    def start_res(d, _):
        res_copy(d).start()
        return 0

    lax.fori_loop(1, n, start_res, 0)

    @pl.when(s < n - 1)
    def _():
        gm_copy.wait_recv()

        def halo_grad(cols, _):
            gh[:, cols] = gh[:, cols] + product3(fwd, slice(None), slice(R, N), gm_halo[:, cols])
            return 0

        tiles(WIDE, halo_grad)

    def backward(cols, acc):
        gr, gi = gh[:H, cols], gh[H:, cols]
        fr, fi = fh[:H, cols], fh[H:, cols]
        spectrum = jnp.concatenate([fr * gr + fi * gi, fr * gi - fi * gr], axis=0)
        grad = product3(inv, slice(0, R), slice(None), spectrum)
        value = gain[:, cols] * key[:, cols].astype(F32) * grad
        weighted[:, cols] = value
        return acc + lanes(value * stream[:, cols].astype(F32))

    dots = to_row(tiles(WIDE, backward, jnp.zeros((R, 128), F32)))
    row_send[1] = dots
    for d in range(1, m):
        row_copy(1, d).start()

    def add_rs(d, total):
        rs_copy(d).wait_recv()
        return total + rs_recv[d - 1]

    scale = token_total**-0.5
    ag[s] = lax.fori_loop(1, n, add_rs, gf[s]) * scale

    def ag_copy(d):
        return copy(ag.at[s], ag.at[s], ag_sem, d - 1, (lax.rem(s + d, n), c))

    def start_ag(d, _):
        ag_copy(d).start()
        return 0

    lax.fori_loop(1, n, start_ag, 0)

    for d in range(1, m):
        row_copy(1, d).wait_recv()
        dots = dots + row_recv[1, d - 1]
    dots_col = to_col(dots / channel_total)

    def finish(cols, _):
        scale_rows = wide(inv_col[...])
        pull = wide(inv_col[...] * inv_col[...] * dots_col)
        value = weighted[:, cols] - stream[:, cols].astype(F32) * pull
        out_stream[:, cols] = (scale_rows * value).astype(BF16)
        return 0

    tiles(WIDE, finish)

    def arrived(d, _):
        res_copy(d).wait_recv()
        ag_copy(d).wait_recv()
        return 0

    lax.fori_loop(1, n, arrived, 0)
    out_residue[...] = (
        lax.fori_loop(0, n, lambda i, total: total + res_all[i], jnp.zeros((1, C), F32)) * scale
    )
    for i in range(n):
        out_filter[i * chunk : (i + 1) * chunk, :] = ag[i]

    for d in range(1, m):
        row_copy(0, d).wait_send()
        row_copy(1, d).wait_send()

    @pl.when(s < n - 1)
    def _():
        halo_copy.wait_send()
        inv_copy.wait_send()

    @pl.when(s > 0)
    def _():
        gm_copy.wait_send()

    def carry_sent(d, _):
        carry_copy(d).wait_send()
        return 0

    lax.fori_loop(1, s + 1, carry_sent, 0)

    def sent(d, _):
        rs_copy(d).wait_send()
        ag_copy(d).wait_send()
        res_copy(d).wait_send()
        return 0

    lax.fori_loop(1, n, sent, 0)


def solution(mesh):
    n, m = mesh.shape["seq"], mesh.shape["chan"]

    def body(
        stream,
        norm_gain,
        gate_query,
        gate_key,
        gate_out,
        cotangent,
        medium_filter,
        long_residue,
        long_rate,
    ):
        R, C = stream.shape
        K = medium_filter.shape[0]
        N = R + K
        mats = [jnp.asarray(mat) for mat in transforms(R, K)]
        vmem = pl.BlockSpec(memory_space=pltpu.VMEM)

        def buffer(*shape):
            return pltpu.VMEM(shape, F32)

        def sems(count):
            return pltpu.SemaphoreType.DMA((2, count))

        outs = pl.pallas_call(
            functools.partial(kernel, n, m),
            out_shape=(
                jax.ShapeDtypeStruct((R, C), BF16),
                jax.ShapeDtypeStruct((R, C), BF16),
                jax.ShapeDtypeStruct((K, C), F32),
                jax.ShapeDtypeStruct((1, C), F32),
            ),
            in_specs=[vmem] * 12,
            out_specs=(vmem,) * 4,
            scratch_shapes=[
                buffer(R, C),
                buffer(1, C),
                buffer(R, C),
                buffer(R, C),
                buffer(K, C),
                buffer(K, C),
                buffer(R, 128),
                buffer(3, 8, R),
                buffer(2, m - 1, 8, R),
                buffer(8, R),
                buffer(1, C),
                buffer(n - 1, 1, C),
                buffer(N, C),
                buffer(N, C),
                buffer(N, C),
                buffer(n, K // n, C),
                buffer(n - 1, K // n, C),
                buffer(n, K // n, C),
                buffer(n, 1, C),
                buffer(R, C),
                sems(3),
                sems(2 * (m - 1)),
                sems(n - 1),
                sems(n - 1),
                sems(n - 1),
                sems(n - 1),
            ],
            compiler_params=pltpu.CompilerParams(
                collective_id=0, has_side_effects=True, vmem_limit_bytes=48 * 2**20
            ),
            cost_estimate=pl.CostEstimate(
                flops=2 * (2 * N + 2 * R + 2 * K) * N * C * 3,
                bytes_accessed=8 * R * C * 2,
                transcendentals=R * C,
            ),
        )(
            stream,
            norm_gain[None],
            gate_query,
            gate_key,
            gate_out,
            cotangent,
            medium_filter,
            long_residue[None],
            long_rate[None],
            *mats,
        )
        return outs[0], outs[1], outs[2], outs[3][0]

    in_specs = (
        P("seq", "chan"),
        P("chan"),
        P("seq", "chan"),
        P("seq", "chan"),
        P("seq", "chan"),
        P("seq", "chan"),
        P(None, "chan"),
        P("chan"),
        P("chan"),
    )
    out_specs = (P("seq", "chan"), P("seq", "chan"), P(None, "chan"), P("chan"))
    return jax.shard_map(body, mesh=mesh, in_specs=in_specs, out_specs=out_specs, check_vma=False)
```

```python
import functools

import jax
import jax.numpy as jnp
import ml_dtypes
import numpy as np
from jax import lax
from jax.experimental import pallas as pl
from jax.experimental.pallas import tpu as pltpu
from jax.sharding import PartitionSpec as P

EPSILON = 1e-05
F32 = jnp.float32
BF16 = jnp.bfloat16
MESH = pl.DeviceIdType.MESH
WIDE = 256


def split_np(matrix):
    high = matrix.astype(ml_dtypes.bfloat16)
    low = (matrix - high.astype(np.float64)).astype(ml_dtypes.bfloat16)
    return np.stack([high, low])


def transforms(rows, taps):
    length = rows + taps
    freqs = np.arange(length // 2)[:, None] * 2 + 1
    turns = (freqs * np.arange(length)[None, :]) % (2 * length)
    angle = np.pi * turns / length
    forward = np.concatenate([np.cos(angle), -np.sin(angle)], axis=0)
    inverse = forward.T * (2.0 / length)
    lags = inverse[taps - np.arange(taps)]
    return split_np(forward), split_np(inverse), split_np(lags)


def halves(value):
    high = value.astype(BF16)
    low = (value - high.astype(F32)).astype(BF16)
    return high, low


def product3(mat_ref, rows, cols, value):
    high, low = halves(value)
    mat_high = mat_ref[0, rows, cols]
    mat_low = mat_ref[1, rows, cols]
    total = jnp.dot(mat_high, high, preferred_element_type=F32)
    total += jnp.dot(mat_low, high, preferred_element_type=F32)
    return total + jnp.dot(mat_high, low, preferred_element_type=F32)


def kernel(
    n,
    m,
    stream_hbm,
    gain_hbm,
    query_hbm,
    key_hbm,
    gate_out_hbm,
    cotangent_hbm,
    taps_hbm,
    residue_hbm,
    rate_hbm,
    fwd_hbm,
    inv_hbm,
    lag_hbm,
    out_query,
    out_stream,
    out_filter,
    out_residue,
    stream,
    gain,
    query,
    key,
    gate_out,
    cotangent,
    taps_ref,
    residue,
    rate,
    fwd,
    inv,
    lag,
    raw,
    entering,
    rev,
    gm,
    raw_halo,
    gm_halo,
    inv_col,
    row_send,
    row_recv,
    inv_halo,
    carry_send,
    carry_recv,
    fh,
    xh,
    gh,
    gf,
    rs_recv,
    part,
    ex_recv,
    ag,
    res_all,
    weighted,
    load_sem,
    inv_sem,
    halo_sem,
    gm_sem,
    row_sem,
    carry_sem,
    rs_sem,
    ex_sem,
    ag_sem,
    res_sem,
):
    s, c = lax.axis_index("seq"), lax.axis_index("chan")
    R, C = stream.shape
    K = taps_ref.shape[0]
    N = R + K
    H = N // 2
    T, A, chunk, _ = gf.shape
    B = n // A
    a, b = lax.div(s, B), lax.rem(s, B)
    channel_total = C * m
    token_total = R * n
    head, tail = pl.ds(0, R - K), pl.ds(R - K, K)

    loads = {}

    def load(name, src, dst):
        loads[name] = pltpu.make_async_copy(src, dst, load_sem.at[len(loads)])
        loads[name].start()

    load("gain", gain_hbm, gain)
    load("stream_tail", stream_hbm.at[tail, :], stream.at[tail, :])
    load("key_tail", key_hbm.at[tail, :], key.at[tail, :])
    load("stream_head", stream_hbm.at[head, :], stream.at[head, :])
    load("key_head", key_hbm.at[head, :], key.at[head, :])
    load("rate", rate_hbm, rate)
    load("gate_out", gate_out_hbm, gate_out)
    load("cotangent", cotangent_hbm, cotangent)
    load("fwd", fwd_hbm, fwd)
    load("taps", taps_hbm, taps_ref)
    load("residue", residue_hbm, residue)
    load("query", query_hbm, query)
    load("lag", lag_hbm, lag)
    load("inv", inv_hbm, inv)

    barrier = pltpu.get_barrier_semaphore()

    def greet(d, _):
        pl.semaphore_signal(barrier, inc=1, device_id=(lax.rem(s + d, n), c), device_id_type=MESH)
        return 0

    lax.fori_loop(1, n, greet, 0)
    for d in range(1, m):
        pl.semaphore_signal(barrier, inc=1, device_id=(s, lax.rem(c + d, m)), device_id_type=MESH)

    def tiles(width, step, init=0):
        def run(i, carry):
            return step(i, pl.ds(pl.multiple_of(i * width, width), width), carry)

        return lax.fori_loop(0, C // width, run, init)

    def lanes(value):
        return sum(value[:, i * 128 : (i + 1) * 128] for i in range(value.shape[1] // 128))

    def wide(col):
        return jnp.concatenate([col] * (WIDE // 128), axis=1)

    def to_row(acc):
        return jnp.broadcast_to(jnp.sum(acc.T, axis=0, keepdims=True), (8, R))

    def to_col(row):
        return jnp.broadcast_to(row[0:1, :], (128, R)).T

    def copy(src, dst, sems, index, target):
        return pltpu.make_async_remote_copy(
            src_ref=src,
            dst_ref=dst,
            send_sem=sems.at[0, index],
            recv_sem=sems.at[1, index],
            device_id=target,
            device_id_type=MESH,
        )

    after = (lax.rem(s + 1, n), c)
    before = (lax.rem(s + n - 1, n), c)

    def halo_copy(i, cols):
        return copy(raw.at[tail, cols], raw_halo.at[:, cols], halo_sem, i, after)

    def gm_copy(i, cols):
        return copy(gm.at[pl.ds(0, K), cols], gm_halo.at[:, cols], gm_sem, i, before)

    inv_copy = copy(row_send.at[2], inv_halo, inv_sem, 0, after)

    def row_copy(kind, d):
        return copy(
            row_send.at[kind],
            row_recv.at[kind, d - 1],
            row_sem,
            kind * (m - 1) + d - 1,
            (s, lax.rem(c + d, m)),
        )

    def gated(rows, cols, acc):
        x = stream[rows, cols].astype(F32)
        raw[rows, cols] = key[rows, cols].astype(F32) * x * gain[:, cols]
        return acc + lanes(x * x)

    loads["gain"].wait()
    loads["stream_tail"].wait()
    loads["key_tail"].wait()
    squares_tail = tiles(
        WIDE, lambda i, cols, acc: gated(tail, cols, acc), jnp.zeros((K, 128), F32)
    )
    pl.semaphore_wait(barrier, n - 1 + m - 1)

    @pl.when(s < n - 1)
    def _():
        def start(i, cols, _):
            halo_copy(i, cols).start()
            return 0

        tiles(WIDE, start)

    loads["stream_head"].wait()
    loads["key_head"].wait()
    squares_head = tiles(
        WIDE, lambda i, cols, acc: gated(head, cols, acc), jnp.zeros((R - K, 128), F32)
    )
    squares = to_row(jnp.concatenate([squares_head, squares_tail], axis=0))
    row_send[0] = squares
    for d in range(1, m):
        row_copy(0, d).start()

    loads["rate"].wait()
    loads["gate_out"].wait()
    loads["cotangent"].wait()

    def recur(i, cols, _):
        value = gate_out[:, cols].astype(F32) * cotangent[:, cols].astype(F32)
        slow = rate[:, cols]
        row = lax.broadcasted_iota(jnp.int32, value.shape, 0)
        k = 1
        while k < R:
            factor = jnp.exp(-slow * k)
            if k < 8:
                moved = jnp.where(row < R - k, pltpu.roll(value, R - k, 0), 0.0)
            else:
                moved = jnp.concatenate([value[k:], jnp.zeros((k, value.shape[1]), F32)], axis=0)
            value = value + factor * moved
            k *= 2
        rev[:, cols] = value
        carry_send[:, cols] = value[0:1]
        return 0

    tiles(128, recur)

    def carry_copy(d):
        return copy(
            carry_send, carry_recv.at[d - 1], carry_sem, d - 1, (lax.rem(s + n - d, n), c)
        )

    def start_carry(d, _):
        carry_copy(d).start()
        return 0

    lax.fori_loop(1, s + 1, start_carry, 0)

    loads["fwd"].wait()
    loads["taps"].wait()

    def tap_spectrum(i, cols, _):
        fh[:, cols] = product3(fwd, slice(None), slice(0, K), taps_ref[:, cols])
        return 0

    tiles(WIDE, tap_spectrum)

    loads["residue"].wait()
    loads["query"].wait()

    def wait_carry(d, _):
        carry_copy(d).wait_recv()
        return 0

    lax.fori_loop(1, n - s, wait_carry, 0)
    block_decay = jnp.exp(-rate[...] * R)

    def horner(i, later):
        return block_decay * later + carry_recv[n - 2 - s - i]

    entering[...] = lax.fori_loop(0, n - 1 - s, horner, jnp.zeros((1, C), F32))

    def norm_factor(slow):
        z = 2.0 * slow
        poly = 1.0 - z / 6.0
        for k in (5.0, 4.0, 3.0, 2.0):
            poly = 1.0 - z / k * poly
        return jnp.sqrt(z * poly)

    def state(i, cols, _):
        slow = rate[:, cols]
        position = lax.broadcasted_iota(jnp.int32, (R, WIDE), 0).astype(F32)
        value = rev[:, cols] + jnp.exp(-slow * (R - position)) * entering[:, cols]
        rev[:, cols] = value
        gm[:, cols] = query[:, cols].astype(F32) * (residue[:, cols] * norm_factor(slow) * value)

        @pl.when(s > 0)
        def _():
            gm_copy(i, cols).start()

        return 0

    tiles(WIDE, state)

    total = squares
    for d in range(1, m):
        row_copy(0, d).wait_recv()
        total = total + row_recv[0, d - 1]
    inv_row = lax.rsqrt(total / channel_total + EPSILON)
    row_send[2] = inv_row
    inv_col[...] = to_col(inv_row)

    @pl.when(s < n - 1)
    def _():
        inv_copy.start()

    def local_spectra(i, cols, _):
        gh[:, cols] = product3(fwd, slice(None), slice(0, R), gm[:, cols])
        value = raw[:, cols] * wide(inv_col[...])
        xh[:, cols] = product3(fwd, slice(None), slice(K, N), value)
        return 0

    tiles(WIDE, local_spectra)

    @pl.when(s > 0)
    def _():
        inv_copy.wait_recv()

    loads["lag"].wait()
    loads["inv"].wait()

    def at_line(d):
        return (lax.rem(a + d, A) * B + b, c)

    def rs_copy(i, d):
        return copy(
            gf.at[i, lax.rem(a + d, A)],
            rs_recv.at[i, d - 1],
            rs_sem,
            i * (A - 1) + d - 1,
            at_line(d),
        )

    def forward(i, cols, _):
        @pl.when(s > 0)
        def _():
            halo_copy(i, cols).wait_recv()
            halo = raw_halo[:, cols] * wide(to_col(inv_halo[...])[R - K :])
            xh[:, cols] = xh[:, cols] + product3(fwd, slice(None), slice(0, K), halo)

        xr, xi = xh[:H, cols], xh[H:, cols]
        gr, gi = gh[:H, cols], gh[H:, cols]
        spectrum = jnp.concatenate([gr * xr + gi * xi, gr * xi - gi * xr], axis=0)
        value = product3(lag, slice(None), slice(None), spectrum)
        for k in range(A):
            gf[i, k] = value[k * chunk : (k + 1) * chunk]

        def start(d, _):
            rs_copy(i, d).start()
            return 0

        lax.fori_loop(1, A, start, 0)

        fr, fi = fh[:H, cols], fh[H:, cols]
        spectrum = jnp.concatenate([fr * xr - fi * xi, fr * xi + fi * xr], axis=0)
        mixed = product3(inv, slice(K, N), slice(None), spectrum)
        factor = norm_factor(rate[:, cols])
        states = rev[:, cols]
        out_query[:, cols] = (mixed * (residue[:, cols] * factor * states)).astype(BF16)
        stored = (query[:, cols].astype(F32) * mixed).astype(BF16).astype(F32)
        res_all[s, :, cols] = factor * jnp.sum(stored * states, axis=0, keepdims=True)
        return 0

    tiles(WIDE, forward)

    def res_copy(d):
        return copy(res_all.at[s], res_all.at[s], res_sem, d - 1, (lax.rem(s + d, n), c))

    def start_res(d, _):
        res_copy(d).start()
        return 0

    lax.fori_loop(1, n, start_res, 0)

    def ex_copy(i):
        return copy(part.at[i], ex_recv.at[i], ex_sem, i, (a * B + (B - 1 - b), c))

    def ag_copy(i, d):
        return copy(ag.at[i, a], ag.at[i, a], ag_sem, i * (A - 1) + d - 1, at_line(d))

    def add_line(i, _):
        def add(d, total):
            rs_copy(i, d).wait_recv()
            return total + rs_recv[i, d - 1]

        part[i] = lax.fori_loop(1, A, add, gf[i, a])
        if B == 2:
            ex_copy(i).start()
        return 0

    lax.fori_loop(0, T, add_line, 0)
    scale = token_total**-0.5

    def add_partner(i, _):
        total = part[i]
        if B == 2:
            ex_copy(i).wait_recv()
            total = total + ex_recv[i]
        ag[i, a] = total * scale

        def start(d, _):
            ag_copy(i, d).start()
            return 0

        lax.fori_loop(1, A, start, 0)
        return 0

    lax.fori_loop(0, T, add_partner, 0)

    def backward(i, cols, acc):
        @pl.when(s < n - 1)
        def _():
            gm_copy(i, cols).wait_recv()
            gh[:, cols] = gh[:, cols] + product3(fwd, slice(None), slice(R, N), gm_halo[:, cols])

        gr, gi = gh[:H, cols], gh[H:, cols]
        fr, fi = fh[:H, cols], fh[H:, cols]
        spectrum = jnp.concatenate([fr * gr + fi * gi, fr * gi - fi * gr], axis=0)
        grad = product3(inv, slice(0, R), slice(None), spectrum)
        value = gain[:, cols] * key[:, cols].astype(F32) * grad
        weighted[:, cols] = value
        return acc + lanes(value * stream[:, cols].astype(F32))

    dots = to_row(tiles(WIDE, backward, jnp.zeros((R, 128), F32)))
    row_send[1] = dots
    for d in range(1, m):
        row_copy(1, d).start()
    for d in range(1, m):
        row_copy(1, d).wait_recv()
        dots = dots + row_recv[1, d - 1]
    dots_col = to_col(dots / channel_total)

    def finish(i, cols, _):
        scale_rows = wide(inv_col[...])
        pull = wide(inv_col[...] * inv_col[...] * dots_col)
        value = weighted[:, cols] - stream[:, cols].astype(F32) * pull
        out_stream[:, cols] = (scale_rows * value).astype(BF16)
        return 0

    tiles(WIDE, finish)

    def res_arrived(d, _):
        res_copy(d).wait_recv()
        return 0

    lax.fori_loop(1, n, res_arrived, 0)
    out_residue[...] = (
        lax.fori_loop(0, n, lambda i, total: total + res_all[i], jnp.zeros((1, C), F32)) * scale
    )

    def spread(i, cols, _):
        def arrived(d, _):
            ag_copy(i, d).wait_recv()
            return 0

        lax.fori_loop(1, A, arrived, 0)
        for k in range(A):
            out_filter[k * chunk : (k + 1) * chunk, cols] = ag[i, k]
        return 0

    tiles(WIDE, spread)

    for d in range(1, m):
        row_copy(0, d).wait_send()
        row_copy(1, d).wait_send()

    def left(i, cols, _):
        @pl.when(s < n - 1)
        def _():
            halo_copy(i, cols).wait_send()

        @pl.when(s > 0)
        def _():
            gm_copy(i, cols).wait_send()

        if B == 2:
            ex_copy(i).wait_send()

        def line(d, _):
            rs_copy(i, d).wait_send()
            ag_copy(i, d).wait_send()
            return 0

        lax.fori_loop(1, A, line, 0)
        return 0

    tiles(WIDE, left)

    @pl.when(s < n - 1)
    def _():
        inv_copy.wait_send()

    def carry_sent(d, _):
        carry_copy(d).wait_send()
        return 0

    lax.fori_loop(1, s + 1, carry_sent, 0)

    def res_sent(d, _):
        res_copy(d).wait_send()
        return 0

    lax.fori_loop(1, n, res_sent, 0)


def solution(mesh):
    n, m = mesh.shape["seq"], mesh.shape["chan"]

    def body(
        stream,
        norm_gain,
        gate_query,
        gate_key,
        gate_out,
        cotangent,
        medium_filter,
        long_residue,
        long_rate,
    ):
        R, C = stream.shape
        K = medium_filter.shape[0]
        N = R + K
        mats = [jnp.asarray(mat) for mat in transforms(R, K)]
        T = C // WIDE
        B = 2 if n % 2 == 0 else 1
        A = n // B
        vmem = pl.BlockSpec(memory_space=pltpu.VMEM)
        hbm = pl.BlockSpec(memory_space=pltpu.HBM)

        def buffer(*shape):
            return pltpu.VMEM(shape, F32)

        def sems(count):
            return pltpu.SemaphoreType.DMA((2, count))

        outs = pl.pallas_call(
            functools.partial(kernel, n, m),
            out_shape=(
                jax.ShapeDtypeStruct((R, C), BF16),
                jax.ShapeDtypeStruct((R, C), BF16),
                jax.ShapeDtypeStruct((K, C), F32),
                jax.ShapeDtypeStruct((1, C), F32),
            ),
            in_specs=[hbm] * 12,
            out_specs=(vmem,) * 4,
            scratch_shapes=[
                pltpu.VMEM((R, C), BF16),
                buffer(1, C),
                pltpu.VMEM((R, C), BF16),
                pltpu.VMEM((R, C), BF16),
                pltpu.VMEM((R, C), BF16),
                pltpu.VMEM((R, C), BF16),
                buffer(K, C),
                buffer(1, C),
                buffer(1, C),
                *(pltpu.VMEM(mat.shape, BF16) for mat in mats),
                buffer(R, C),
                buffer(1, C),
                buffer(R, C),
                buffer(R, C),
                buffer(K, C),
                buffer(K, C),
                buffer(R, 128),
                buffer(3, 8, R),
                buffer(2, m - 1, 8, R),
                buffer(8, R),
                buffer(1, C),
                buffer(n - 1, 1, C),
                buffer(N, C),
                buffer(N, C),
                buffer(N, C),
                buffer(T, A, K // A, WIDE),
                buffer(T, A - 1, K // A, WIDE),
                buffer(T, K // A, WIDE),
                buffer(T, K // A, WIDE),
                buffer(T, A, K // A, WIDE),
                buffer(n, 1, C),
                buffer(R, C),
                pltpu.SemaphoreType.DMA((14,)),
                sems(1),
                sems(T),
                sems(T),
                sems(2 * (m - 1)),
                sems(n - 1),
                sems(T * (A - 1)),
                sems(T),
                sems(T * (A - 1)),
                sems(n - 1),
            ],
            compiler_params=pltpu.CompilerParams(
                collective_id=0, has_side_effects=True, vmem_limit_bytes=48 * 2**20
            ),
            cost_estimate=pl.CostEstimate(
                flops=2 * (2 * N + 2 * R + 2 * K) * N * C * 3,
                bytes_accessed=8 * R * C * 2,
                transcendentals=R * C,
            ),
        )(
            stream,
            norm_gain[None],
            gate_query,
            gate_key,
            gate_out,
            cotangent,
            medium_filter,
            long_residue[None],
            long_rate[None],
            *mats,
        )
        return outs[0], outs[1], outs[2], outs[3][0]

    in_specs = (
        P("seq", "chan"),
        P("chan"),
        P("seq", "chan"),
        P("seq", "chan"),
        P("seq", "chan"),
        P("seq", "chan"),
        P(None, "chan"),
        P("chan"),
        P("chan"),
    )
    out_specs = (P("seq", "chan"), P("seq", "chan"), P(None, "chan"), P("chan"))
    return jax.shard_map(body, mesh=mesh, in_specs=in_specs, out_specs=out_specs, check_vma=False)
```

```python
import functools

import jax
import jax.numpy as jnp
import ml_dtypes
import numpy as np
from jax import lax
from jax.experimental import pallas as pl
from jax.experimental.pallas import tpu as pltpu
from jax.sharding import PartitionSpec as P

EPSILON = 1e-05
F32 = jnp.float32
BF16 = jnp.bfloat16
MESH = pl.DeviceIdType.MESH
WIDE = 256


def split_np(matrix):
    high = matrix.astype(ml_dtypes.bfloat16)
    low = (matrix - high.astype(np.float64)).astype(ml_dtypes.bfloat16)
    return np.stack([high, low])


def transforms(rows, taps):
    length = rows + taps
    freqs = np.arange(length // 2)[:, None] * 2 + 1
    turns = (freqs * np.arange(length)[None, :]) % (2 * length)
    angle = np.pi * turns / length
    forward = np.concatenate([np.cos(angle), -np.sin(angle)], axis=0)
    inverse = forward.T * (2.0 / length)
    lags = inverse[taps - np.arange(taps)]
    return split_np(forward), split_np(inverse), split_np(lags)


def halves(value):
    high = value.astype(BF16)
    low = (value - high.astype(F32)).astype(BF16)
    return high, low


def product3(mat_ref, rows, cols, value):
    high, low = halves(value)
    mat_high = mat_ref[0, rows, cols]
    mat_low = mat_ref[1, rows, cols]
    total = jnp.dot(mat_high, high, preferred_element_type=F32)
    total += jnp.dot(mat_low, high, preferred_element_type=F32)
    return total + jnp.dot(mat_high, low, preferred_element_type=F32)


def kernel(
    n,
    m,
    stream_hbm,
    gain_hbm,
    query_hbm,
    key_hbm,
    gate_out_hbm,
    cotangent_hbm,
    taps_hbm,
    residue_hbm,
    rate_hbm,
    fwd_hbm,
    inv_hbm,
    lag_hbm,
    out_query,
    out_stream,
    out_filter,
    out_residue,
    stream,
    gain,
    query,
    key,
    gate_out,
    cotangent,
    taps_ref,
    residue,
    rate,
    fwd,
    inv,
    lag,
    raw,
    entering,
    rev,
    gm,
    raw_halo,
    gm_halo,
    inv_col,
    row_send,
    row_recv,
    inv_halo,
    carry_send,
    carry_recv,
    fh,
    xh,
    gh,
    gf,
    rs_recv,
    part,
    ex_recv,
    ag,
    res_all,
    weighted,
    load_sem,
    inv_sem,
    halo_sem,
    gm_sem,
    row_sem,
    carry_sem,
    rs_sem,
    ex_sem,
    ag_sem,
    res_sem,
):
    s, c = lax.axis_index("seq"), lax.axis_index("chan")
    R, C = stream.shape
    K = taps_ref.shape[0]
    N = R + K
    H = N // 2
    T, A, chunk, _ = gf.shape
    B = n // A
    a, b = lax.div(s, B), lax.rem(s, B)
    channel_total = C * m
    token_total = R * n
    head, tail = pl.ds(0, R - K), pl.ds(R - K, K)

    loads = {}

    def load(name, src, dst):
        loads[name] = pltpu.make_async_copy(src, dst, load_sem.at[len(loads)])
        loads[name].start()

    load("gain", gain_hbm, gain)
    load("stream_tail", stream_hbm.at[tail, :], stream.at[tail, :])
    load("key_tail", key_hbm.at[tail, :], key.at[tail, :])
    load("stream_head", stream_hbm.at[head, :], stream.at[head, :])
    load("key_head", key_hbm.at[head, :], key.at[head, :])
    load("rate", rate_hbm, rate)
    load("gate_out", gate_out_hbm, gate_out)
    load("cotangent", cotangent_hbm, cotangent)
    load("fwd", fwd_hbm, fwd)
    load("taps", taps_hbm, taps_ref)
    load("residue", residue_hbm, residue)
    load("query", query_hbm, query)
    load("lag", lag_hbm, lag)
    load("inv", inv_hbm, inv)

    barrier = pltpu.get_barrier_semaphore()

    def greet(d, _):
        pl.semaphore_signal(barrier, inc=1, device_id=(lax.rem(s + d, n), c), device_id_type=MESH)
        return 0

    lax.fori_loop(1, n, greet, 0)
    for d in range(1, m):
        pl.semaphore_signal(barrier, inc=1, device_id=(s, lax.rem(c + d, m)), device_id_type=MESH)

    def tiles(width, step, init=0):
        def run(i, carry):
            return step(i, pl.ds(pl.multiple_of(i * width, width), width), carry)

        return lax.fori_loop(0, C // width, run, init)

    def lanes(value):
        return sum(value[:, i * 128 : (i + 1) * 128] for i in range(value.shape[1] // 128))

    def wide(col):
        return jnp.concatenate([col] * (WIDE // 128), axis=1)

    def to_row(acc):
        return jnp.broadcast_to(jnp.sum(acc.T, axis=0, keepdims=True), (8, R))

    def to_col(row):
        return jnp.broadcast_to(row[0:1, :], (128, R)).T

    def copy(src, dst, sems, index, target):
        return pltpu.make_async_remote_copy(
            src_ref=src,
            dst_ref=dst,
            send_sem=sems.at[0, index],
            recv_sem=sems.at[1, index],
            device_id=target,
            device_id_type=MESH,
        )

    after = (lax.rem(s + 1, n), c)
    before = (lax.rem(s + n - 1, n), c)

    def halo_copy(i, cols):
        return copy(raw.at[tail, cols], raw_halo.at[:, cols], halo_sem, i, after)

    def gm_copy(i, cols):
        return copy(gm.at[pl.ds(0, K), cols], gm_halo.at[:, cols], gm_sem, i, before)

    inv_copy = copy(row_send.at[2], inv_halo, inv_sem, 0, after)

    def row_copy(kind, d):
        return copy(
            row_send.at[kind],
            row_recv.at[kind, d - 1],
            row_sem,
            kind * (m - 1) + d - 1,
            (s, lax.rem(c + d, m)),
        )

    def gated(rows, cols, acc):
        x = stream[rows, cols].astype(F32)
        raw[rows, cols] = key[rows, cols].astype(F32) * x * gain[:, cols]
        return acc + lanes(x * x)

    loads["gain"].wait()
    loads["stream_tail"].wait()
    loads["key_tail"].wait()
    squares_tail = tiles(
        WIDE, lambda i, cols, acc: gated(tail, cols, acc), jnp.zeros((K, 128), F32)
    )
    pl.semaphore_wait(barrier, n - 1 + m - 1)

    @pl.when(s < n - 1)
    def _():
        def start(i, cols, _):
            halo_copy(i, cols).start()
            return 0

        tiles(WIDE, start)

    loads["stream_head"].wait()
    loads["key_head"].wait()
    squares_head = tiles(
        WIDE, lambda i, cols, acc: gated(head, cols, acc), jnp.zeros((R - K, 128), F32)
    )
    squares = to_row(jnp.concatenate([squares_head, squares_tail], axis=0))
    row_send[0] = squares
    for d in range(1, m):
        row_copy(0, d).start()

    loads["rate"].wait()
    loads["gate_out"].wait()
    loads["cotangent"].wait()

    def recur(i, cols, _):
        value = gate_out[:, cols].astype(F32) * cotangent[:, cols].astype(F32)
        slow = rate[:, cols]
        row = lax.broadcasted_iota(jnp.int32, value.shape, 0)
        k = 1
        while k < R:
            factor = jnp.exp(-slow * k)
            if k < 8:
                moved = jnp.where(row < R - k, pltpu.roll(value, R - k, 0), 0.0)
            else:
                moved = jnp.concatenate([value[k:], jnp.zeros((k, value.shape[1]), F32)], axis=0)
            value = value + factor * moved
            k *= 2
        rev[:, cols] = value
        carry_send[:, cols] = value[0:1]
        return 0

    tiles(128, recur)

    def carry_copy(d):
        return copy(
            carry_send, carry_recv.at[d - 1], carry_sem, d - 1, (lax.rem(s + n - d, n), c)
        )

    def start_carry(d, _):
        carry_copy(d).start()
        return 0

    lax.fori_loop(1, s + 1, start_carry, 0)

    loads["fwd"].wait()
    loads["taps"].wait()

    def tap_spectrum(i, cols, _):
        fh[:, cols] = product3(fwd, slice(None), slice(0, K), taps_ref[:, cols])
        return 0

    tiles(WIDE, tap_spectrum)

    loads["residue"].wait()
    loads["query"].wait()

    def wait_carry(d, _):
        carry_copy(d).wait_recv()
        return 0

    lax.fori_loop(1, n - s, wait_carry, 0)
    block_decay = jnp.exp(-rate[...] * R)

    def horner(i, later):
        return block_decay * later + carry_recv[n - 2 - s - i]

    entering[...] = lax.fori_loop(0, n - 1 - s, horner, jnp.zeros((1, C), F32))

    def norm_factor(slow):
        z = 2.0 * slow
        poly = 1.0 - z / 6.0
        for k in (5.0, 4.0, 3.0, 2.0):
            poly = 1.0 - z / k * poly
        return jnp.sqrt(z * poly)

    def state(i, cols, _):
        slow = rate[:, cols]
        position = lax.broadcasted_iota(jnp.int32, (R, WIDE), 0).astype(F32)
        value = rev[:, cols] + jnp.exp(-slow * (R - position)) * entering[:, cols]
        rev[:, cols] = value
        gm[:, cols] = query[:, cols].astype(F32) * (residue[:, cols] * norm_factor(slow) * value)
        return 0

    tiles(WIDE, state)

    total = squares
    for d in range(1, m):
        row_copy(0, d).wait_recv()
        total = total + row_recv[0, d - 1]
    inv_row = lax.rsqrt(total / channel_total + EPSILON)
    row_send[2] = inv_row
    inv_col[...] = to_col(inv_row)

    @pl.when(s < n - 1)
    def _():
        inv_copy.start()

    def local_spectra(i, cols, _):
        gh[:, cols] = product3(fwd, slice(None), slice(0, R), gm[:, cols])
        value = raw[:, cols] * wide(inv_col[...])
        xh[:, cols] = product3(fwd, slice(None), slice(K, N), value)
        return 0

    tiles(WIDE, local_spectra)

    @pl.when(s > 0)
    def _():
        inv_copy.wait_recv()

    loads["lag"].wait()
    loads["inv"].wait()

    def at_line(d):
        return (lax.rem(a + d, A) * B + b, c)

    def rs_copy(i, d):
        return copy(
            gf.at[i, lax.rem(a + d, A)],
            rs_recv.at[i, d - 1],
            rs_sem,
            i * (A - 1) + d - 1,
            at_line(d),
        )

    def forward(i, cols, _):
        @pl.when(s > 0)
        def _():
            halo_copy(i, cols).wait_recv()
            halo = raw_halo[:, cols] * wide(to_col(inv_halo[...])[R - K :])
            xh[:, cols] = xh[:, cols] + product3(fwd, slice(None), slice(0, K), halo)

        xr, xi = xh[:H, cols], xh[H:, cols]
        gr, gi = gh[:H, cols], gh[H:, cols]
        spectrum = jnp.concatenate([gr * xr + gi * xi, gr * xi - gi * xr], axis=0)
        value = product3(lag, slice(None), slice(None), spectrum)
        for k in range(A):
            gf[i, k] = value[k * chunk : (k + 1) * chunk]

        def start(d, _):
            rs_copy(i, d).start()
            return 0

        lax.fori_loop(1, A, start, 0)

        @pl.when(s > 0)
        def _():
            gm_copy(i, cols).start()

        fr, fi = fh[:H, cols], fh[H:, cols]
        spectrum = jnp.concatenate([fr * xr - fi * xi, fr * xi + fi * xr], axis=0)
        mixed = product3(inv, slice(K, N), slice(None), spectrum)
        factor = norm_factor(rate[:, cols])
        states = rev[:, cols]
        out_query[:, cols] = (mixed * (residue[:, cols] * factor * states)).astype(BF16)
        stored = (query[:, cols].astype(F32) * mixed).astype(BF16).astype(F32)
        res_all[s, :, cols] = factor * jnp.sum(stored * states, axis=0, keepdims=True)
        return 0

    tiles(WIDE, forward)

    def res_copy(d):
        return copy(res_all.at[s], res_all.at[s], res_sem, d - 1, (lax.rem(s + d, n), c))

    def start_res(d, _):
        res_copy(d).start()
        return 0

    lax.fori_loop(1, n, start_res, 0)

    def ex_copy(i):
        return copy(part.at[i], ex_recv.at[i], ex_sem, i, (a * B + (B - 1 - b), c))

    def ag_copy(i, d):
        return copy(ag.at[i, a], ag.at[i, a], ag_sem, i * (A - 1) + d - 1, at_line(d))

    def add_line(i, _):
        def add(d, total):
            rs_copy(i, d).wait_recv()
            return total + rs_recv[i, d - 1]

        part[i] = lax.fori_loop(1, A, add, gf[i, a])
        if B == 2:
            ex_copy(i).start()
        return 0

    lax.fori_loop(0, T, add_line, 0)
    scale = token_total**-0.5

    def add_partner(i, _):
        total = part[i]
        if B == 2:
            ex_copy(i).wait_recv()
            total = total + ex_recv[i]
        ag[i, a] = total * scale

        def start(d, _):
            ag_copy(i, d).start()
            return 0

        lax.fori_loop(1, A, start, 0)
        return 0

    lax.fori_loop(0, T, add_partner, 0)

    def backward(i, cols, acc):
        @pl.when(s < n - 1)
        def _():
            gm_copy(i, cols).wait_recv()
            gh[:, cols] = gh[:, cols] + product3(fwd, slice(None), slice(R, N), gm_halo[:, cols])

        gr, gi = gh[:H, cols], gh[H:, cols]
        fr, fi = fh[:H, cols], fh[H:, cols]
        spectrum = jnp.concatenate([fr * gr + fi * gi, fr * gi - fi * gr], axis=0)
        grad = product3(inv, slice(0, R), slice(None), spectrum)
        value = gain[:, cols] * key[:, cols].astype(F32) * grad
        weighted[:, cols] = value
        return acc + lanes(value * stream[:, cols].astype(F32))

    dots = to_row(tiles(WIDE, backward, jnp.zeros((R, 128), F32)))
    row_send[1] = dots
    for d in range(1, m):
        row_copy(1, d).start()
    for d in range(1, m):
        row_copy(1, d).wait_recv()
        dots = dots + row_recv[1, d - 1]
    dots_col = to_col(dots / channel_total)

    def finish(i, cols, _):
        scale_rows = wide(inv_col[...])
        pull = wide(inv_col[...] * inv_col[...] * dots_col)
        value = weighted[:, cols] - stream[:, cols].astype(F32) * pull
        out_stream[:, cols] = (scale_rows * value).astype(BF16)
        return 0

    tiles(WIDE, finish)

    def res_arrived(d, _):
        res_copy(d).wait_recv()
        return 0

    lax.fori_loop(1, n, res_arrived, 0)
    out_residue[...] = (
        lax.fori_loop(0, n, lambda i, total: total + res_all[i], jnp.zeros((1, C), F32)) * scale
    )

    def spread(i, cols, _):
        def arrived(d, _):
            ag_copy(i, d).wait_recv()
            return 0

        lax.fori_loop(1, A, arrived, 0)
        for k in range(A):
            out_filter[k * chunk : (k + 1) * chunk, cols] = ag[i, k]
        return 0

    tiles(WIDE, spread)

    for d in range(1, m):
        row_copy(0, d).wait_send()
        row_copy(1, d).wait_send()

    def left(i, cols, _):
        @pl.when(s < n - 1)
        def _():
            halo_copy(i, cols).wait_send()

        @pl.when(s > 0)
        def _():
            gm_copy(i, cols).wait_send()

        if B == 2:
            ex_copy(i).wait_send()

        def line(d, _):
            rs_copy(i, d).wait_send()
            ag_copy(i, d).wait_send()
            return 0

        lax.fori_loop(1, A, line, 0)
        return 0

    tiles(WIDE, left)

    @pl.when(s < n - 1)
    def _():
        inv_copy.wait_send()

    def carry_sent(d, _):
        carry_copy(d).wait_send()
        return 0

    lax.fori_loop(1, s + 1, carry_sent, 0)

    def res_sent(d, _):
        res_copy(d).wait_send()
        return 0

    lax.fori_loop(1, n, res_sent, 0)


def solution(mesh):
    n, m = mesh.shape["seq"], mesh.shape["chan"]

    def body(
        stream,
        norm_gain,
        gate_query,
        gate_key,
        gate_out,
        cotangent,
        medium_filter,
        long_residue,
        long_rate,
    ):
        R, C = stream.shape
        K = medium_filter.shape[0]
        N = R + K
        mats = [jnp.asarray(mat) for mat in transforms(R, K)]
        T = C // WIDE
        B = 2 if n % 2 == 0 else 1
        A = n // B
        vmem = pl.BlockSpec(memory_space=pltpu.VMEM)
        hbm = pl.BlockSpec(memory_space=pltpu.HBM)

        def buffer(*shape):
            return pltpu.VMEM(shape, F32)

        def sems(count):
            return pltpu.SemaphoreType.DMA((2, count))

        outs = pl.pallas_call(
            functools.partial(kernel, n, m),
            out_shape=(
                jax.ShapeDtypeStruct((R, C), BF16),
                jax.ShapeDtypeStruct((R, C), BF16),
                jax.ShapeDtypeStruct((K, C), F32),
                jax.ShapeDtypeStruct((1, C), F32),
            ),
            in_specs=[hbm] * 12,
            out_specs=(vmem,) * 4,
            scratch_shapes=[
                pltpu.VMEM((R, C), BF16),
                buffer(1, C),
                pltpu.VMEM((R, C), BF16),
                pltpu.VMEM((R, C), BF16),
                pltpu.VMEM((R, C), BF16),
                pltpu.VMEM((R, C), BF16),
                buffer(K, C),
                buffer(1, C),
                buffer(1, C),
                *(pltpu.VMEM(mat.shape, BF16) for mat in mats),
                buffer(R, C),
                buffer(1, C),
                buffer(R, C),
                buffer(R, C),
                buffer(K, C),
                buffer(K, C),
                buffer(R, 128),
                buffer(3, 8, R),
                buffer(2, m - 1, 8, R),
                buffer(8, R),
                buffer(1, C),
                buffer(n - 1, 1, C),
                buffer(N, C),
                buffer(N, C),
                buffer(N, C),
                buffer(T, A, K // A, WIDE),
                buffer(T, A - 1, K // A, WIDE),
                buffer(T, K // A, WIDE),
                buffer(T, K // A, WIDE),
                buffer(T, A, K // A, WIDE),
                buffer(n, 1, C),
                buffer(R, C),
                pltpu.SemaphoreType.DMA((14,)),
                sems(1),
                sems(T),
                sems(T),
                sems(2 * (m - 1)),
                sems(n - 1),
                sems(T * (A - 1)),
                sems(T),
                sems(T * (A - 1)),
                sems(n - 1),
            ],
            compiler_params=pltpu.CompilerParams(
                collective_id=0, has_side_effects=True, vmem_limit_bytes=62 * 2**20
            ),
            cost_estimate=pl.CostEstimate(
                flops=2 * (2 * N + 2 * R + 2 * K) * N * C * 3,
                bytes_accessed=8 * R * C * 2,
                transcendentals=R * C,
            ),
        )(
            stream,
            norm_gain[None],
            gate_query,
            gate_key,
            gate_out,
            cotangent,
            medium_filter,
            long_residue[None],
            long_rate[None],
            *mats,
        )
        return outs[0], outs[1], outs[2], outs[3][0]

    in_specs = (
        P("seq", "chan"),
        P("chan"),
        P("seq", "chan"),
        P("seq", "chan"),
        P("seq", "chan"),
        P("seq", "chan"),
        P(None, "chan"),
        P("chan"),
        P("chan"),
    )
    out_specs = (P("seq", "chan"), P("seq", "chan"), P(None, "chan"), P("chan"))
    return jax.shard_map(body, mesh=mesh, in_specs=in_specs, out_specs=out_specs, check_vma=False)
```

```python
import functools

import jax
import jax.numpy as jnp
import ml_dtypes
import numpy as np
from jax import lax
from jax.experimental import pallas as pl
from jax.experimental.pallas import tpu as pltpu
from jax.sharding import PartitionSpec as P

EPSILON = 1e-05
F32 = jnp.float32
BF16 = jnp.bfloat16
MESH = pl.DeviceIdType.MESH
WIDE = 256


def split_np(matrix):
    high = matrix.astype(ml_dtypes.bfloat16)
    low = (matrix - high.astype(np.float64)).astype(ml_dtypes.bfloat16)
    return np.stack([high, low])


def transforms(rows, taps):
    length = rows + taps
    freqs = np.arange(length // 2)[:, None] * 2 + 1
    turns = (freqs * np.arange(length)[None, :]) % (2 * length)
    angle = np.pi * turns / length
    forward = np.concatenate([np.cos(angle), -np.sin(angle)], axis=0)
    inverse = forward.T * (2.0 / length)
    lags = inverse[taps - np.arange(taps)]
    return split_np(forward), split_np(inverse), split_np(lags)


def halves(value):
    high = value.astype(BF16)
    low = (value - high.astype(F32)).astype(BF16)
    return high, low


def product3(mat_ref, rows, cols, value):
    high, low = halves(value)
    mat_high = mat_ref[0, rows, cols]
    mat_low = mat_ref[1, rows, cols]
    total = jnp.dot(mat_high, high, preferred_element_type=F32)
    total += jnp.dot(mat_low, high, preferred_element_type=F32)
    return total + jnp.dot(mat_high, low, preferred_element_type=F32)


def kernel(
    n,
    m,
    stream_hbm,
    gain_hbm,
    query_hbm,
    key_hbm,
    gate_out_hbm,
    cotangent_hbm,
    taps_hbm,
    residue_hbm,
    rate_hbm,
    fwd_hbm,
    inv_hbm,
    lag_hbm,
    out_query,
    out_stream,
    out_filter,
    out_residue,
    stream,
    gain,
    query,
    key,
    gate_out,
    cotangent,
    taps_ref,
    residue,
    rate,
    fwd,
    inv,
    lag,
    raw,
    entering,
    rev,
    gm,
    raw_halo,
    gm_halo,
    inv_col,
    row_send,
    row_recv,
    inv_halo,
    carry_send,
    carry_recv,
    fh,
    xh,
    gh,
    gf,
    rs_recv,
    part,
    ex_recv,
    ag,
    res_all,
    weighted,
    load_sem,
    inv_sem,
    halo_sem,
    gm_sem,
    row_sem,
    carry_sem,
    rs_sem,
    ex_sem,
    ag_sem,
    fwd_sem,
    res_sem,
):
    s, c = lax.axis_index("seq"), lax.axis_index("chan")
    R, C = stream.shape
    K = taps_ref.shape[0]
    N = R + K
    H = N // 2
    T, A, chunk, _ = gf.shape
    B = n // A
    a, b = lax.div(s, B), lax.rem(s, B)
    channel_total = C * m
    token_total = R * n
    head, tail = pl.ds(0, R - K), pl.ds(R - K, K)

    loads = {}

    def load(name, src, dst):
        loads[name] = pltpu.make_async_copy(src, dst, load_sem.at[len(loads)])
        loads[name].start()

    load("gain", gain_hbm, gain)
    load("stream_tail", stream_hbm.at[tail, :], stream.at[tail, :])
    load("key_tail", key_hbm.at[tail, :], key.at[tail, :])
    load("stream_head", stream_hbm.at[head, :], stream.at[head, :])
    load("key_head", key_hbm.at[head, :], key.at[head, :])
    load("rate", rate_hbm, rate)
    load("gate_out", gate_out_hbm, gate_out)
    load("cotangent", cotangent_hbm, cotangent)
    load("fwd", fwd_hbm, fwd)
    load("taps", taps_hbm, taps_ref)
    load("residue", residue_hbm, residue)
    load("query", query_hbm, query)
    load("lag", lag_hbm, lag)
    load("inv", inv_hbm, inv)

    barrier = pltpu.get_barrier_semaphore()

    def greet(d, _):
        pl.semaphore_signal(barrier, inc=1, device_id=(lax.rem(s + d, n), c), device_id_type=MESH)
        return 0

    lax.fori_loop(1, n, greet, 0)
    for d in range(1, m):
        pl.semaphore_signal(barrier, inc=1, device_id=(s, lax.rem(c + d, m)), device_id_type=MESH)

    def tiles(width, step, init=0):
        def run(i, carry):
            return step(i, pl.ds(pl.multiple_of(i * width, width), width), carry)

        return lax.fori_loop(0, C // width, run, init)

    def lanes(value):
        return sum(value[:, i * 128 : (i + 1) * 128] for i in range(value.shape[1] // 128))

    def wide(col):
        return jnp.concatenate([col] * (WIDE // 128), axis=1)

    def to_row(acc):
        return jnp.broadcast_to(jnp.sum(acc.T, axis=0, keepdims=True), (8, R))

    def to_col(row):
        return jnp.broadcast_to(row[0:1, :], (128, R)).T

    def copy(src, dst, sems, index, target):
        return pltpu.make_async_remote_copy(
            src_ref=src,
            dst_ref=dst,
            send_sem=sems.at[0, index],
            recv_sem=sems.at[1, index],
            device_id=target,
            device_id_type=MESH,
        )

    after = (lax.rem(s + 1, n), c)
    before = (lax.rem(s + n - 1, n), c)

    def halo_copy(i, cols):
        return copy(raw.at[tail, cols], raw_halo.at[:, cols], halo_sem, i, after)

    def gm_copy(i, cols):
        return copy(gm.at[pl.ds(0, K), cols], gm_halo.at[:, cols], gm_sem, i, before)

    inv_copy = copy(row_send.at[2], inv_halo, inv_sem, 0, after)

    def row_copy(kind, d):
        return copy(
            row_send.at[kind],
            row_recv.at[kind, d - 1],
            row_sem,
            kind * (m - 1) + d - 1,
            (s, lax.rem(c + d, m)),
        )

    def gated(rows, cols, acc):
        x = stream[rows, cols].astype(F32)
        raw[rows, cols] = key[rows, cols].astype(F32) * x * gain[:, cols]
        return acc + lanes(x * x)

    loads["gain"].wait()
    loads["stream_tail"].wait()
    loads["key_tail"].wait()
    squares_tail = tiles(
        WIDE, lambda i, cols, acc: gated(tail, cols, acc), jnp.zeros((K, 128), F32)
    )
    pl.semaphore_wait(barrier, n - 1 + m - 1)

    @pl.when(s < n - 1)
    def _():
        def start(i, cols, _):
            halo_copy(i, cols).start()
            return 0

        tiles(WIDE, start)

    loads["stream_head"].wait()
    loads["key_head"].wait()
    squares_head = tiles(
        WIDE, lambda i, cols, acc: gated(head, cols, acc), jnp.zeros((R - K, 128), F32)
    )
    squares = to_row(jnp.concatenate([squares_head, squares_tail], axis=0))
    row_send[0] = squares
    for d in range(1, m):
        row_copy(0, d).start()

    loads["rate"].wait()
    loads["gate_out"].wait()
    loads["cotangent"].wait()

    def recur(i, cols, _):
        value = gate_out[:, cols].astype(F32) * cotangent[:, cols].astype(F32)
        slow = rate[:, cols]
        row = lax.broadcasted_iota(jnp.int32, value.shape, 0)
        k = 1
        while k < R:
            factor = jnp.exp(-slow * k)
            if k < 8:
                moved = jnp.where(row < R - k, pltpu.roll(value, R - k, 0), 0.0)
            else:
                moved = jnp.concatenate([value[k:], jnp.zeros((k, value.shape[1]), F32)], axis=0)
            value = value + factor * moved
            k *= 2
        rev[:, cols] = value
        carry_send[:, cols] = value[0:1]
        return 0

    tiles(128, recur)

    def carry_copy(d):
        return copy(
            carry_send, carry_recv.at[d - 1], carry_sem, d - 1, (lax.rem(s + n - d, n), c)
        )

    def start_carry(d, _):
        carry_copy(d).start()
        return 0

    lax.fori_loop(1, s + 1, start_carry, 0)

    loads["fwd"].wait()
    loads["taps"].wait()

    def tap_spectrum(i, cols, _):
        fh[:, cols] = product3(fwd, slice(None), slice(0, K), taps_ref[:, cols])
        return 0

    tiles(WIDE, tap_spectrum)

    loads["residue"].wait()
    loads["query"].wait()

    def wait_carry(d, _):
        carry_copy(d).wait_recv()
        return 0

    lax.fori_loop(1, n - s, wait_carry, 0)
    block_decay = jnp.exp(-rate[...] * R)

    def horner(i, later):
        return block_decay * later + carry_recv[n - 2 - s - i]

    entering[...] = lax.fori_loop(0, n - 1 - s, horner, jnp.zeros((1, C), F32))

    def norm_factor(slow):
        z = 2.0 * slow
        poly = 1.0 - z / 6.0
        for k in (5.0, 4.0, 3.0, 2.0):
            poly = 1.0 - z / k * poly
        return jnp.sqrt(z * poly)

    def state(i, cols, _):
        slow = rate[:, cols]
        position = lax.broadcasted_iota(jnp.int32, (R, WIDE), 0).astype(F32)
        value = rev[:, cols] + jnp.exp(-slow * (R - position)) * entering[:, cols]
        rev[:, cols] = value
        gm[:, cols] = query[:, cols].astype(F32) * (residue[:, cols] * norm_factor(slow) * value)
        return 0

    tiles(WIDE, state)

    total = squares
    for d in range(1, m):
        row_copy(0, d).wait_recv()
        total = total + row_recv[0, d - 1]
    inv_row = lax.rsqrt(total / channel_total + EPSILON)
    row_send[2] = inv_row
    inv_col[...] = to_col(inv_row)

    @pl.when(s < n - 1)
    def _():
        inv_copy.start()

    def local_spectra(i, cols, _):
        gh[:, cols] = product3(fwd, slice(None), slice(0, R), gm[:, cols])
        value = raw[:, cols] * wide(inv_col[...])
        xh[:, cols] = product3(fwd, slice(None), slice(K, N), value)
        return 0

    tiles(WIDE, local_spectra)

    @pl.when(s > 0)
    def _():
        inv_copy.wait_recv()

    loads["lag"].wait()
    loads["inv"].wait()

    def at_line(d):
        return (lax.rem(a + d, A) * B + b, c)

    def rs_copy(i, d):
        return copy(
            gf.at[i, lax.rem(a + d, A)],
            rs_recv.at[i, d - 1],
            rs_sem,
            i * (A - 1) + d - 1,
            at_line(d),
        )

    def forward(i, cols, _):
        @pl.when(s > 0)
        def _():
            halo_copy(i, cols).wait_recv()
            halo = raw_halo[:, cols] * wide(to_col(inv_halo[...])[R - K :])
            xh[:, cols] = xh[:, cols] + product3(fwd, slice(None), slice(0, K), halo)

        xr, xi = xh[:H, cols], xh[H:, cols]
        gr, gi = gh[:H, cols], gh[H:, cols]
        spectrum = jnp.concatenate([gr * xr + gi * xi, gr * xi - gi * xr], axis=0)
        value = product3(lag, slice(None), slice(None), spectrum)
        for k in range(A):
            gf[i, k] = value[k * chunk : (k + 1) * chunk]

        def start(d, _):
            rs_copy(i, d).start()
            return 0

        lax.fori_loop(1, A, start, 0)

        @pl.when(s > 0)
        def _():
            gm_copy(i, cols).start()

        fr, fi = fh[:H, cols], fh[H:, cols]
        spectrum = jnp.concatenate([fr * xr - fi * xi, fr * xi + fi * xr], axis=0)
        mixed = product3(inv, slice(K, N), slice(None), spectrum)
        factor = norm_factor(rate[:, cols])
        states = rev[:, cols]
        out_query[:, cols] = (mixed * (residue[:, cols] * factor * states)).astype(BF16)
        stored = (query[:, cols].astype(F32) * mixed).astype(BF16).astype(F32)
        res_all[s, :, cols] = factor * jnp.sum(stored * states, axis=0, keepdims=True)
        return 0

    tiles(WIDE, forward)

    def res_copy(d):
        return copy(res_all.at[s], res_all.at[s], res_sem, d - 1, (lax.rem(s + d, n), c))

    def start_res(d, _):
        res_copy(d).start()
        return 0

    lax.fori_loop(1, n, start_res, 0)

    def ex_copy(i):
        return copy(part.at[i], ex_recv.at[i], ex_sem, i, (a * B + (B - 1 - b), c))

    def ag_copy(i, d):
        return copy(ag.at[i, a], ag.at[i, a], ag_sem, i * (A - 1) + d - 1, at_line(d))

    def add_line(i, _):
        def add(d, total):
            rs_copy(i, d).wait_recv()
            return total + rs_recv[i, d - 1]

        part[i] = lax.fori_loop(1, A, add, gf[i, a])

        @pl.when(lax.rem(i, B) != b)
        def _():
            ex_copy(i).start()

        return 0

    lax.fori_loop(0, T, add_line, 0)
    scale = token_total**-0.5

    def fwd_copy(i):
        return copy(ag.at[i], ag.at[i], fwd_sem, i, (a * B + (B - 1 - b), c))

    def add_partner(i, _):
        @pl.when(lax.rem(i, B) == b)
        def _():
            total = part[i]
            if B == 2:
                ex_copy(i).wait_recv()
                total = total + ex_recv[i]
            ag[i, a] = total * scale

            def start(d, _):
                ag_copy(i, d).start()
                return 0

            lax.fori_loop(1, A, start, 0)

        return 0

    lax.fori_loop(0, T, add_partner, 0)

    def backward(i, cols, acc):
        @pl.when(s < n - 1)
        def _():
            gm_copy(i, cols).wait_recv()
            gh[:, cols] = gh[:, cols] + product3(fwd, slice(None), slice(R, N), gm_halo[:, cols])

        gr, gi = gh[:H, cols], gh[H:, cols]
        fr, fi = fh[:H, cols], fh[H:, cols]
        spectrum = jnp.concatenate([fr * gr + fi * gi, fr * gi - fi * gr], axis=0)
        grad = product3(inv, slice(0, R), slice(None), spectrum)
        value = gain[:, cols] * key[:, cols].astype(F32) * grad
        weighted[:, cols] = value
        return acc + lanes(value * stream[:, cols].astype(F32))

    dots = to_row(tiles(WIDE, backward, jnp.zeros((R, 128), F32)))
    row_send[1] = dots
    for d in range(1, m):
        row_copy(1, d).start()

    def gathered(i, _):
        @pl.when(lax.rem(i, B) == b)
        def _():
            def arrived(d, _):
                ag_copy(i, d).wait_recv()
                return 0

            lax.fori_loop(1, A, arrived, 0)
            if B == 2:
                fwd_copy(i).start()

        return 0

    lax.fori_loop(0, T, gathered, 0)
    for d in range(1, m):
        row_copy(1, d).wait_recv()
        dots = dots + row_recv[1, d - 1]
    dots_col = to_col(dots / channel_total)

    def finish(i, cols, _):
        scale_rows = wide(inv_col[...])
        pull = wide(inv_col[...] * inv_col[...] * dots_col)
        value = weighted[:, cols] - stream[:, cols].astype(F32) * pull
        out_stream[:, cols] = (scale_rows * value).astype(BF16)
        return 0

    tiles(WIDE, finish)

    def res_arrived(d, _):
        res_copy(d).wait_recv()
        return 0

    lax.fori_loop(1, n, res_arrived, 0)
    out_residue[...] = (
        lax.fori_loop(0, n, lambda i, total: total + res_all[i], jnp.zeros((1, C), F32)) * scale
    )

    def spread(i, cols, _):
        @pl.when(lax.rem(i, B) != b)
        def _():
            fwd_copy(i).wait_recv()

        for k in range(A):
            out_filter[k * chunk : (k + 1) * chunk, cols] = ag[i, k]
        return 0

    tiles(WIDE, spread)

    for d in range(1, m):
        row_copy(0, d).wait_send()
        row_copy(1, d).wait_send()

    def left(i, cols, _):
        @pl.when(s < n - 1)
        def _():
            halo_copy(i, cols).wait_send()

        @pl.when(s > 0)
        def _():
            gm_copy(i, cols).wait_send()

        def line(d, _):
            rs_copy(i, d).wait_send()
            return 0

        lax.fori_loop(1, A, line, 0)

        @pl.when(lax.rem(i, B) != b)
        def _():
            ex_copy(i).wait_send()

        @pl.when(lax.rem(i, B) == b)
        def _():
            def line(d, _):
                ag_copy(i, d).wait_send()
                return 0

            lax.fori_loop(1, A, line, 0)
            if B == 2:
                fwd_copy(i).wait_send()

        return 0

    tiles(WIDE, left)

    @pl.when(s < n - 1)
    def _():
        inv_copy.wait_send()

    def carry_sent(d, _):
        carry_copy(d).wait_send()
        return 0

    lax.fori_loop(1, s + 1, carry_sent, 0)

    def res_sent(d, _):
        res_copy(d).wait_send()
        return 0

    lax.fori_loop(1, n, res_sent, 0)


def hand_over(*refs):
    sem = refs[8]
    copies = [pltpu.make_async_copy(refs[i], refs[4 + i], sem.at[i]) for i in range(4)]
    for one in copies:
        one.start()
    for one in copies:
        one.wait()


def solution(mesh):
    n, m = mesh.shape["seq"], mesh.shape["chan"]

    def body(
        stream,
        norm_gain,
        gate_query,
        gate_key,
        gate_out,
        cotangent,
        medium_filter,
        long_residue,
        long_rate,
    ):
        R, C = stream.shape
        K = medium_filter.shape[0]
        N = R + K
        mats = [jnp.asarray(mat) for mat in transforms(R, K)]
        T = C // WIDE
        B = 2 if n % 2 == 0 else 1
        A = n // B
        vmem = pl.BlockSpec(memory_space=pltpu.VMEM)
        hbm = pl.BlockSpec(memory_space=pltpu.HBM)

        def buffer(*shape):
            return pltpu.VMEM(shape, F32)

        def sems(count):
            return pltpu.SemaphoreType.DMA((2, count))

        outs = pl.pallas_call(
            functools.partial(kernel, n, m),
            out_shape=(
                jax.ShapeDtypeStruct((R, C), BF16),
                jax.ShapeDtypeStruct((R, C), BF16),
                jax.ShapeDtypeStruct((K, C), F32),
                jax.ShapeDtypeStruct((1, C), F32),
            ),
            in_specs=[hbm] * 12,
            out_specs=(vmem,) * 4,
            scratch_shapes=[
                pltpu.VMEM((R, C), BF16),
                buffer(1, C),
                pltpu.VMEM((R, C), BF16),
                pltpu.VMEM((R, C), BF16),
                pltpu.VMEM((R, C), BF16),
                pltpu.VMEM((R, C), BF16),
                buffer(K, C),
                buffer(1, C),
                buffer(1, C),
                *(pltpu.VMEM(mat.shape, BF16) for mat in mats),
                buffer(R, C),
                buffer(1, C),
                buffer(R, C),
                buffer(R, C),
                buffer(K, C),
                buffer(K, C),
                buffer(R, 128),
                buffer(3, 8, R),
                buffer(2, m - 1, 8, R),
                buffer(8, R),
                buffer(1, C),
                buffer(n - 1, 1, C),
                buffer(N, C),
                buffer(N, C),
                buffer(N, C),
                buffer(T, A, K // A, WIDE),
                buffer(T, A - 1, K // A, WIDE),
                buffer(T, K // A, WIDE),
                buffer(T, K // A, WIDE),
                buffer(T, A, K // A, WIDE),
                buffer(n, 1, C),
                buffer(R, C),
                pltpu.SemaphoreType.DMA((14,)),
                sems(1),
                sems(T),
                sems(T),
                sems(2 * (m - 1)),
                sems(n - 1),
                sems(T * (A - 1)),
                sems(T),
                sems(T * (A - 1)),
                sems(T),
                sems(n - 1),
            ],
            compiler_params=pltpu.CompilerParams(
                collective_id=0, has_side_effects=True, vmem_limit_bytes=62 * 2**20
            ),
            cost_estimate=pl.CostEstimate(
                flops=2 * (2 * N + 2 * R + 2 * K) * N * C * 3,
                bytes_accessed=8 * R * C * 2,
                transcendentals=R * C,
            ),
        )(
            stream,
            norm_gain[None],
            gate_query,
            gate_key,
            gate_out,
            cotangent,
            medium_filter,
            long_residue[None],
            long_rate[None],
            *mats,
        )
        outs = pl.pallas_call(
            hand_over,
            out_shape=tuple(jax.ShapeDtypeStruct(out.shape, out.dtype) for out in outs),
            in_specs=[hbm] * 4,
            out_specs=(hbm,) * 4,
            scratch_shapes=[pltpu.SemaphoreType.DMA((4,))],
            compiler_params=pltpu.CompilerParams(vmem_limit_bytes=62 * 2**20),
        )(*outs)
        return outs[0], outs[1], outs[2], outs[3][0]

    in_specs = (
        P("seq", "chan"),
        P("chan"),
        P("seq", "chan"),
        P("seq", "chan"),
        P("seq", "chan"),
        P("seq", "chan"),
        P(None, "chan"),
        P("chan"),
        P("chan"),
    )
    out_specs = (P("seq", "chan"), P("seq", "chan"), P(None, "chan"), P("chan"))
    return jax.shard_map(body, mesh=mesh, in_specs=in_specs, out_specs=out_specs, check_vma=False)
```

```python
import functools

import jax
import jax.numpy as jnp
import ml_dtypes
import numpy as np
from jax import lax
from jax.experimental import pallas as pl
from jax.experimental.pallas import tpu as pltpu
from jax.sharding import PartitionSpec as P

EPSILON = 1e-05
F32 = jnp.float32
BF16 = jnp.bfloat16
MESH = pl.DeviceIdType.MESH
WIDE = 256


def split_np(matrix):
    high = matrix.astype(ml_dtypes.bfloat16)
    low = (matrix - high.astype(np.float64)).astype(ml_dtypes.bfloat16)
    return np.stack([high, low])


def transforms(rows, taps):
    length = rows + taps
    freqs = np.arange(length // 2)[:, None] * 2 + 1
    turns = (freqs * np.arange(length)[None, :]) % (2 * length)
    angle = np.pi * turns / length
    forward = np.concatenate([np.cos(angle), -np.sin(angle)], axis=0)
    inverse = forward.T * (2.0 / length)
    lags = inverse[taps - np.arange(taps)]
    return split_np(forward), split_np(inverse), split_np(lags)


def product2(mat_ref, rows, cols, value):
    value = value.astype(BF16)
    total = jnp.dot(mat_ref[0, rows, cols], value, preferred_element_type=F32)
    return total + jnp.dot(mat_ref[1, rows, cols], value, preferred_element_type=F32)


def kernel(
    n,
    m,
    stream_hbm,
    gain_hbm,
    query_hbm,
    key_hbm,
    gate_out_hbm,
    cotangent_hbm,
    taps_hbm,
    residue_hbm,
    rate_hbm,
    fwd_hbm,
    inv_hbm,
    lag_hbm,
    out_query,
    out_stream,
    out_filter,
    out_residue,
    stream,
    gain,
    query,
    key,
    gate_out,
    cotangent,
    taps_ref,
    residue,
    rate,
    fwd,
    inv,
    lag,
    raw,
    entering,
    rev,
    gm,
    raw_halo,
    gm_halo,
    inv_col,
    row_send,
    row_recv,
    inv_halo,
    carry_send,
    carry_recv,
    fh,
    xh,
    gh,
    gf,
    rs_recv,
    part,
    ex_recv,
    ag,
    res_all,
    weighted,
    load_sem,
    inv_sem,
    halo_sem,
    gm_sem,
    row_sem,
    carry_sem,
    rs_sem,
    ex_sem,
    ag_sem,
    fwd_sem,
    res_sem,
):
    s, c = lax.axis_index("seq"), lax.axis_index("chan")
    R, C = stream.shape
    K = taps_ref.shape[0]
    N = R + K
    H = N // 2
    T, A, chunk, _ = gf.shape
    B = n // A
    a, b = lax.div(s, B), lax.rem(s, B)
    channel_total = C * m
    token_total = R * n
    head, tail = pl.ds(0, R - K), pl.ds(R - K, K)

    loads = {}

    def load(name, src, dst):
        loads[name] = pltpu.make_async_copy(src, dst, load_sem.at[len(loads)])
        loads[name].start()

    load("gain", gain_hbm, gain)
    load("stream_tail", stream_hbm.at[tail, :], stream.at[tail, :])
    load("key_tail", key_hbm.at[tail, :], key.at[tail, :])
    load("stream_head", stream_hbm.at[head, :], stream.at[head, :])
    load("key_head", key_hbm.at[head, :], key.at[head, :])
    load("rate", rate_hbm, rate)
    load("gate_out", gate_out_hbm, gate_out)
    load("cotangent", cotangent_hbm, cotangent)
    load("fwd", fwd_hbm, fwd)
    load("taps", taps_hbm, taps_ref)
    load("residue", residue_hbm, residue)
    load("query", query_hbm, query)
    load("lag", lag_hbm, lag)
    load("inv", inv_hbm, inv)

    barrier = pltpu.get_barrier_semaphore()

    def greet(d, _):
        pl.semaphore_signal(barrier, inc=1, device_id=(lax.rem(s + d, n), c), device_id_type=MESH)
        return 0

    lax.fori_loop(1, n, greet, 0)
    for d in range(1, m):
        pl.semaphore_signal(barrier, inc=1, device_id=(s, lax.rem(c + d, m)), device_id_type=MESH)

    def tiles(width, step, init=0):
        def run(i, carry):
            return step(i, pl.ds(pl.multiple_of(i * width, width), width), carry)

        return lax.fori_loop(0, C // width, run, init)

    def lanes(value):
        return sum(value[:, i * 128 : (i + 1) * 128] for i in range(value.shape[1] // 128))

    def wide(col):
        return jnp.concatenate([col] * (WIDE // 128), axis=1)

    def to_row(acc):
        return jnp.broadcast_to(jnp.sum(acc.T, axis=0, keepdims=True), (8, R))

    def to_col(row):
        return jnp.broadcast_to(row[0:1, :], (128, R)).T

    def copy(src, dst, sems, index, target):
        return pltpu.make_async_remote_copy(
            src_ref=src,
            dst_ref=dst,
            send_sem=sems.at[0, index],
            recv_sem=sems.at[1, index],
            device_id=target,
            device_id_type=MESH,
        )

    after = (lax.rem(s + 1, n), c)
    before = (lax.rem(s + n - 1, n), c)

    def halo_copy(i, cols):
        return copy(raw.at[tail, cols], raw_halo.at[:, cols], halo_sem, i, after)

    def gm_copy(i, cols):
        return copy(gm.at[pl.ds(0, K), cols], gm_halo.at[:, cols], gm_sem, i, before)

    inv_copy = copy(row_send.at[2], inv_halo, inv_sem, 0, after)

    def row_copy(kind, d):
        return copy(
            row_send.at[kind],
            row_recv.at[kind, d - 1],
            row_sem,
            kind * (m - 1) + d - 1,
            (s, lax.rem(c + d, m)),
        )

    def gated(rows, cols, acc):
        x = stream[rows, cols].astype(F32)
        raw[rows, cols] = key[rows, cols].astype(F32) * x * gain[:, cols]
        return acc + lanes(x * x)

    loads["gain"].wait()
    loads["stream_tail"].wait()
    loads["key_tail"].wait()
    squares_tail = tiles(
        WIDE, lambda i, cols, acc: gated(tail, cols, acc), jnp.zeros((K, 128), F32)
    )
    pl.semaphore_wait(barrier, n - 1 + m - 1)

    @pl.when(s < n - 1)
    def _():
        def start(i, cols, _):
            halo_copy(i, cols).start()
            return 0

        tiles(WIDE, start)

    loads["stream_head"].wait()
    loads["key_head"].wait()
    squares_head = tiles(
        WIDE, lambda i, cols, acc: gated(head, cols, acc), jnp.zeros((R - K, 128), F32)
    )
    squares = to_row(jnp.concatenate([squares_head, squares_tail], axis=0))
    row_send[0] = squares
    for d in range(1, m):
        row_copy(0, d).start()

    loads["rate"].wait()
    loads["gate_out"].wait()
    loads["cotangent"].wait()

    def recur(i, cols, _):
        value = gate_out[:, cols].astype(F32) * cotangent[:, cols].astype(F32)
        slow = rate[:, cols]
        row = lax.broadcasted_iota(jnp.int32, value.shape, 0)
        k = 1
        while k < R:
            factor = jnp.exp(-slow * k)
            if k < 8:
                moved = jnp.where(row < R - k, pltpu.roll(value, R - k, 0), 0.0)
            else:
                moved = jnp.concatenate([value[k:], jnp.zeros((k, value.shape[1]), F32)], axis=0)
            value = value + factor * moved
            k *= 2
        rev[:, cols] = value
        carry_send[:, cols] = value[0:1]
        return 0

    tiles(128, recur)

    def carry_copy(d):
        return copy(
            carry_send, carry_recv.at[d - 1], carry_sem, d - 1, (lax.rem(s + n - d, n), c)
        )

    def start_carry(d, _):
        carry_copy(d).start()
        return 0

    lax.fori_loop(1, s + 1, start_carry, 0)

    loads["fwd"].wait()
    loads["taps"].wait()

    def tap_spectrum(i, cols, _):
        fh[:, cols] = product2(fwd, slice(None), slice(0, K), taps_ref[:, cols])
        return 0

    tiles(WIDE, tap_spectrum)

    loads["residue"].wait()
    loads["query"].wait()

    def wait_carry(d, _):
        carry_copy(d).wait_recv()
        return 0

    lax.fori_loop(1, n - s, wait_carry, 0)
    block_decay = jnp.exp(-rate[...] * R)

    def horner(i, later):
        return block_decay * later + carry_recv[n - 2 - s - i]

    entering[...] = lax.fori_loop(0, n - 1 - s, horner, jnp.zeros((1, C), F32))

    def norm_factor(slow):
        z = 2.0 * slow
        poly = 1.0 - z / 6.0
        for k in (5.0, 4.0, 3.0, 2.0):
            poly = 1.0 - z / k * poly
        return jnp.sqrt(z * poly)

    def state(i, cols, _):
        slow = rate[:, cols]
        position = lax.broadcasted_iota(jnp.int32, (R, WIDE), 0).astype(F32)
        value = rev[:, cols] + jnp.exp(-slow * (R - position)) * entering[:, cols]
        rev[:, cols] = value
        gm[:, cols] = query[:, cols].astype(F32) * (residue[:, cols] * norm_factor(slow) * value)
        return 0

    tiles(WIDE, state)

    total = squares
    for d in range(1, m):
        row_copy(0, d).wait_recv()
        total = total + row_recv[0, d - 1]
    inv_row = lax.rsqrt(total / channel_total + EPSILON)
    row_send[2] = inv_row
    inv_col[...] = to_col(inv_row)

    @pl.when(s < n - 1)
    def _():
        inv_copy.start()

    def local_spectra(i, cols, _):
        gh[:, cols] = product2(fwd, slice(None), slice(0, R), gm[:, cols])
        value = raw[:, cols] * wide(inv_col[...])
        xh[:, cols] = product2(fwd, slice(None), slice(K, N), value)
        return 0

    tiles(WIDE, local_spectra)

    @pl.when(s > 0)
    def _():
        inv_copy.wait_recv()

    loads["lag"].wait()
    loads["inv"].wait()

    def at_line(d):
        return (lax.rem(a + d, A) * B + b, c)

    def rs_copy(i, d):
        return copy(
            gf.at[i, lax.rem(a + d, A)],
            rs_recv.at[i, d - 1],
            rs_sem,
            i * (A - 1) + d - 1,
            at_line(d),
        )

    def forward(i, cols, _):
        @pl.when(s > 0)
        def _():
            halo_copy(i, cols).wait_recv()
            halo = raw_halo[:, cols] * wide(to_col(inv_halo[...])[R - K :])
            xh[:, cols] = xh[:, cols] + product2(fwd, slice(None), slice(0, K), halo)

        xr, xi = xh[:H, cols], xh[H:, cols]
        gr, gi = gh[:H, cols], gh[H:, cols]
        spectrum = jnp.concatenate([gr * xr + gi * xi, gr * xi - gi * xr], axis=0)
        value = product2(lag, slice(None), slice(None), spectrum)
        for k in range(A):
            gf[i, k] = value[k * chunk : (k + 1) * chunk]

        def start(d, _):
            rs_copy(i, d).start()
            return 0

        lax.fori_loop(1, A, start, 0)

        @pl.when(s > 0)
        def _():
            gm_copy(i, cols).start()

        fr, fi = fh[:H, cols], fh[H:, cols]
        spectrum = jnp.concatenate([fr * xr - fi * xi, fr * xi + fi * xr], axis=0)
        mixed = product2(inv, slice(K, N), slice(None), spectrum)
        factor = norm_factor(rate[:, cols])
        states = rev[:, cols]
        out_query[:, cols] = (mixed * (residue[:, cols] * factor * states)).astype(BF16)
        stored = (query[:, cols].astype(F32) * mixed).astype(BF16).astype(F32)
        res_all[s, :, cols] = factor * jnp.sum(stored * states, axis=0, keepdims=True)
        return 0

    tiles(WIDE, forward)

    def res_copy(d):
        return copy(res_all.at[s], res_all.at[s], res_sem, d - 1, (lax.rem(s + d, n), c))

    def start_res(d, _):
        res_copy(d).start()
        return 0

    lax.fori_loop(1, n, start_res, 0)

    def ex_copy(i):
        return copy(part.at[i], ex_recv.at[i], ex_sem, i, (a * B + (B - 1 - b), c))

    def ag_copy(i, d):
        return copy(ag.at[i, a], ag.at[i, a], ag_sem, i * (A - 1) + d - 1, at_line(d))

    def add_line(i, _):
        def add(d, total):
            rs_copy(i, d).wait_recv()
            return total + rs_recv[i, d - 1]

        part[i] = lax.fori_loop(1, A, add, gf[i, a])

        @pl.when(lax.rem(i, B) != b)
        def _():
            ex_copy(i).start()

        return 0

    lax.fori_loop(0, T, add_line, 0)
    scale = token_total**-0.5

    def fwd_copy(i):
        return copy(ag.at[i], ag.at[i], fwd_sem, i, (a * B + (B - 1 - b), c))

    def add_partner(i, _):
        @pl.when(lax.rem(i, B) == b)
        def _():
            total = part[i]
            if B == 2:
                ex_copy(i).wait_recv()
                total = total + ex_recv[i]
            ag[i, a] = total * scale

            def start(d, _):
                ag_copy(i, d).start()
                return 0

            lax.fori_loop(1, A, start, 0)

        return 0

    lax.fori_loop(0, T, add_partner, 0)

    def backward(i, cols, acc):
        @pl.when(s < n - 1)
        def _():
            gm_copy(i, cols).wait_recv()
            gh[:, cols] = gh[:, cols] + product2(fwd, slice(None), slice(R, N), gm_halo[:, cols])

        gr, gi = gh[:H, cols], gh[H:, cols]
        fr, fi = fh[:H, cols], fh[H:, cols]
        spectrum = jnp.concatenate([fr * gr + fi * gi, fr * gi - fi * gr], axis=0)
        grad = product2(inv, slice(0, R), slice(None), spectrum)
        value = gain[:, cols] * key[:, cols].astype(F32) * grad
        weighted[:, cols] = value
        return acc + lanes(value * stream[:, cols].astype(F32))

    dots = to_row(tiles(WIDE, backward, jnp.zeros((R, 128), F32)))
    row_send[1] = dots
    for d in range(1, m):
        row_copy(1, d).start()

    def gathered(i, _):
        @pl.when(lax.rem(i, B) == b)
        def _():
            def arrived(d, _):
                ag_copy(i, d).wait_recv()
                return 0

            lax.fori_loop(1, A, arrived, 0)
            if B == 2:
                fwd_copy(i).start()

        return 0

    lax.fori_loop(0, T, gathered, 0)
    for d in range(1, m):
        row_copy(1, d).wait_recv()
        dots = dots + row_recv[1, d - 1]
    dots_col = to_col(dots / channel_total)

    def finish(i, cols, _):
        scale_rows = wide(inv_col[...])
        pull = wide(inv_col[...] * inv_col[...] * dots_col)
        value = weighted[:, cols] - stream[:, cols].astype(F32) * pull
        out_stream[:, cols] = (scale_rows * value).astype(BF16)
        return 0

    tiles(WIDE, finish)

    def res_arrived(d, _):
        res_copy(d).wait_recv()
        return 0

    lax.fori_loop(1, n, res_arrived, 0)
    out_residue[...] = (
        lax.fori_loop(0, n, lambda i, total: total + res_all[i], jnp.zeros((1, C), F32)) * scale
    )

    def spread(i, cols, _):
        @pl.when(lax.rem(i, B) != b)
        def _():
            fwd_copy(i).wait_recv()

        for k in range(A):
            out_filter[k * chunk : (k + 1) * chunk, cols] = ag[i, k]
        return 0

    tiles(WIDE, spread)

    for d in range(1, m):
        row_copy(0, d).wait_send()
        row_copy(1, d).wait_send()

    def left(i, cols, _):
        @pl.when(s < n - 1)
        def _():
            halo_copy(i, cols).wait_send()

        @pl.when(s > 0)
        def _():
            gm_copy(i, cols).wait_send()

        def line(d, _):
            rs_copy(i, d).wait_send()
            return 0

        lax.fori_loop(1, A, line, 0)

        @pl.when(lax.rem(i, B) != b)
        def _():
            ex_copy(i).wait_send()

        @pl.when(lax.rem(i, B) == b)
        def _():
            def line(d, _):
                ag_copy(i, d).wait_send()
                return 0

            lax.fori_loop(1, A, line, 0)
            if B == 2:
                fwd_copy(i).wait_send()

        return 0

    tiles(WIDE, left)

    @pl.when(s < n - 1)
    def _():
        inv_copy.wait_send()

    def carry_sent(d, _):
        carry_copy(d).wait_send()
        return 0

    lax.fori_loop(1, s + 1, carry_sent, 0)

    def res_sent(d, _):
        res_copy(d).wait_send()
        return 0

    lax.fori_loop(1, n, res_sent, 0)


def hand_over(*refs):
    held, sem = refs[8:12], refs[12]
    into = [pltpu.make_async_copy(refs[i], held[i], sem.at[0, i]) for i in range(4)]
    away = [pltpu.make_async_copy(held[i], refs[4 + i], sem.at[1, i]) for i in range(4)]
    for one in into:
        one.start()
    for first, second in zip(into, away):
        first.wait()
        second.start()
    for one in away:
        one.wait()


def solution(mesh):
    n, m = mesh.shape["seq"], mesh.shape["chan"]

    def body(
        stream,
        norm_gain,
        gate_query,
        gate_key,
        gate_out,
        cotangent,
        medium_filter,
        long_residue,
        long_rate,
    ):
        R, C = stream.shape
        K = medium_filter.shape[0]
        N = R + K
        mats = [jnp.asarray(mat) for mat in transforms(R, K)]
        T = C // WIDE
        B = 2 if n % 2 == 0 else 1
        A = n // B
        vmem = pl.BlockSpec(memory_space=pltpu.VMEM)
        hbm = pl.BlockSpec(memory_space=pltpu.HBM)

        def buffer(*shape):
            return pltpu.VMEM(shape, F32)

        def sems(count):
            return pltpu.SemaphoreType.DMA((2, count))

        outs = pl.pallas_call(
            functools.partial(kernel, n, m),
            out_shape=(
                jax.ShapeDtypeStruct((R, C), BF16),
                jax.ShapeDtypeStruct((R, C), BF16),
                jax.ShapeDtypeStruct((K, C), F32),
                jax.ShapeDtypeStruct((1, C), F32),
            ),
            in_specs=[hbm] * 12,
            out_specs=(vmem,) * 4,
            scratch_shapes=[
                pltpu.VMEM((R, C), BF16),
                buffer(1, C),
                pltpu.VMEM((R, C), BF16),
                pltpu.VMEM((R, C), BF16),
                pltpu.VMEM((R, C), BF16),
                pltpu.VMEM((R, C), BF16),
                buffer(K, C),
                buffer(1, C),
                buffer(1, C),
                *(pltpu.VMEM(mat.shape, BF16) for mat in mats),
                buffer(R, C),
                buffer(1, C),
                buffer(R, C),
                buffer(R, C),
                buffer(K, C),
                buffer(K, C),
                buffer(R, 128),
                buffer(3, 8, R),
                buffer(2, m - 1, 8, R),
                buffer(8, R),
                buffer(1, C),
                buffer(n - 1, 1, C),
                buffer(N, C),
                buffer(N, C),
                buffer(N, C),
                buffer(T, A, K // A, WIDE),
                buffer(T, A - 1, K // A, WIDE),
                buffer(T, K // A, WIDE),
                buffer(T, K // A, WIDE),
                buffer(T, A, K // A, WIDE),
                buffer(n, 1, C),
                buffer(R, C),
                pltpu.SemaphoreType.DMA((14,)),
                sems(1),
                sems(T),
                sems(T),
                sems(2 * (m - 1)),
                sems(n - 1),
                sems(T * (A - 1)),
                sems(T),
                sems(T * (A - 1)),
                sems(T),
                sems(n - 1),
            ],
            compiler_params=pltpu.CompilerParams(
                collective_id=0, has_side_effects=True, vmem_limit_bytes=62 * 2**20
            ),
            cost_estimate=pl.CostEstimate(
                flops=2 * (2 * N + 2 * R + 2 * K) * N * C * 2,
                bytes_accessed=8 * R * C * 2,
                transcendentals=R * C,
            ),
        )(
            stream,
            norm_gain[None],
            gate_query,
            gate_key,
            gate_out,
            cotangent,
            medium_filter,
            long_residue[None],
            long_rate[None],
            *mats,
        )
        outs = pl.pallas_call(
            hand_over,
            out_shape=tuple(jax.ShapeDtypeStruct(out.shape, out.dtype) for out in outs),
            in_specs=[hbm] * 4,
            out_specs=(hbm,) * 4,
            scratch_shapes=[
                *(pltpu.VMEM(out.shape, out.dtype) for out in outs),
                pltpu.SemaphoreType.DMA((2, 4)),
            ],
            compiler_params=pltpu.CompilerParams(vmem_limit_bytes=62 * 2**20),
        )(*outs)
        return outs[0], outs[1], outs[2], outs[3][0]

    in_specs = (
        P("seq", "chan"),
        P("chan"),
        P("seq", "chan"),
        P("seq", "chan"),
        P("seq", "chan"),
        P("seq", "chan"),
        P(None, "chan"),
        P("chan"),
        P("chan"),
    )
    out_specs = (P("seq", "chan"), P("seq", "chan"), P(None, "chan"), P("chan"))
    return jax.shard_map(body, mesh=mesh, in_specs=in_specs, out_specs=out_specs, check_vma=False)
```

```python
import functools

import jax
import jax.numpy as jnp
import ml_dtypes
import numpy as np
from jax import lax
from jax.experimental import pallas as pl
from jax.experimental.pallas import tpu as pltpu
from jax.sharding import PartitionSpec as P

EPSILON = 1e-05
F32 = jnp.float32
BF16 = jnp.bfloat16
MESH = pl.DeviceIdType.MESH
WIDE = 256


def split_np(matrix):
    high = matrix.astype(ml_dtypes.bfloat16)
    low = (matrix - high.astype(np.float64)).astype(ml_dtypes.bfloat16)
    return np.stack([high, low])


def transforms(rows, taps):
    length = rows + taps
    freqs = np.arange(length // 2)[:, None] * 2 + 1
    turns = (freqs * np.arange(length)[None, :]) % (2 * length)
    angle = np.pi * turns / length
    forward = np.concatenate([np.cos(angle), -np.sin(angle)], axis=0)
    inverse = forward.T * (2.0 / length)
    lags = inverse[taps - np.arange(taps)]
    return split_np(forward), split_np(inverse), split_np(lags)


def product2(mat_ref, rows, cols, value):
    value = value.astype(BF16)
    total = jnp.dot(mat_ref[0, rows, cols], value, preferred_element_type=F32)
    return total + jnp.dot(mat_ref[1, rows, cols], value, preferred_element_type=F32)


def kernel(
    n,
    m,
    stream_hbm,
    gain_hbm,
    query_hbm,
    key_hbm,
    gate_out_hbm,
    cotangent_hbm,
    taps_hbm,
    residue_hbm,
    rate_hbm,
    fwd_hbm,
    inv_hbm,
    lag_hbm,
    out_query,
    out_stream,
    out_filter,
    out_residue,
    stream,
    gain,
    query,
    key,
    gate_out,
    cotangent,
    taps_ref,
    residue,
    rate,
    fwd,
    inv,
    lag,
    raw,
    entering,
    rev,
    gm,
    raw_halo,
    gm_halo,
    inv_col,
    row_send,
    row_recv,
    inv_halo,
    carry_send,
    carry_recv,
    fh,
    xh,
    gh,
    gf,
    rs_recv,
    part,
    ex_recv,
    ag,
    res_all,
    weighted,
    load_sem,
    inv_sem,
    halo_sem,
    gm_sem,
    row_sem,
    carry_sem,
    rs_sem,
    ex_sem,
    ag_sem,
    fwd_sem,
    res_sem,
):
    s, c = lax.axis_index("seq"), lax.axis_index("chan")
    R, C = stream.shape
    K = taps_ref.shape[0]
    N = R + K
    H = N // 2
    T, A, chunk, _ = gf.shape
    B = n // A
    a, b = lax.div(s, B), lax.rem(s, B)
    channel_total = C * m
    token_total = R * n
    head, tail = pl.ds(0, R - K), pl.ds(R - K, K)

    loads = {}

    def load(name, src, dst):
        loads[name] = pltpu.make_async_copy(src, dst, load_sem.at[len(loads)])
        loads[name].start()

    load("gain", gain_hbm, gain)
    load("stream_tail", stream_hbm.at[tail, :], stream.at[tail, :])
    load("key_tail", key_hbm.at[tail, :], key.at[tail, :])
    load("stream_head", stream_hbm.at[head, :], stream.at[head, :])
    load("key_head", key_hbm.at[head, :], key.at[head, :])
    load("rate", rate_hbm, rate)
    load("gate_out", gate_out_hbm, gate_out)
    load("cotangent", cotangent_hbm, cotangent)
    load("fwd", fwd_hbm, fwd)
    load("taps", taps_hbm, taps_ref)
    load("residue", residue_hbm, residue)
    load("query", query_hbm, query)
    load("lag", lag_hbm, lag)
    load("inv", inv_hbm, inv)

    barrier = pltpu.get_barrier_semaphore()

    def greet(d, _):
        pl.semaphore_signal(barrier, inc=1, device_id=(lax.rem(s + d, n), c), device_id_type=MESH)
        return 0

    lax.fori_loop(1, n, greet, 0)
    for d in range(1, m):
        pl.semaphore_signal(barrier, inc=1, device_id=(s, lax.rem(c + d, m)), device_id_type=MESH)

    def tiles(width, step, init=0):
        def run(i, carry):
            return step(i, pl.ds(pl.multiple_of(i * width, width), width), carry)

        return lax.fori_loop(0, C // width, run, init)

    def lanes(value):
        return sum(value[:, i * 128 : (i + 1) * 128] for i in range(value.shape[1] // 128))

    def wide(col):
        return jnp.concatenate([col] * (WIDE // 128), axis=1)

    def to_row(acc):
        return jnp.broadcast_to(jnp.sum(acc.T, axis=0, keepdims=True), (8, R))

    def to_col(row):
        return jnp.broadcast_to(row[0:1, :], (128, R)).T

    def copy(src, dst, sems, index, target):
        return pltpu.make_async_remote_copy(
            src_ref=src,
            dst_ref=dst,
            send_sem=sems.at[0, index],
            recv_sem=sems.at[1, index],
            device_id=target,
            device_id_type=MESH,
        )

    after = (lax.rem(s + 1, n), c)
    before = (lax.rem(s + n - 1, n), c)

    def halo_copy(i, cols):
        return copy(raw.at[tail, cols], raw_halo.at[:, cols], halo_sem, i, after)

    def gm_copy(i, cols):
        return copy(gm.at[pl.ds(0, K), cols], gm_halo.at[:, cols], gm_sem, i, before)

    inv_copy = copy(row_send.at[2], inv_halo, inv_sem, 0, after)

    def row_copy(kind, d):
        return copy(
            row_send.at[kind],
            row_recv.at[kind, d - 1],
            row_sem,
            kind * (m - 1) + d - 1,
            (s, lax.rem(c + d, m)),
        )

    def gated(rows, cols, acc):
        x = stream[rows, cols].astype(F32)
        raw[rows, cols] = key[rows, cols].astype(F32) * x * gain[:, cols]
        return acc + lanes(x * x)

    loads["gain"].wait()
    loads["stream_tail"].wait()
    loads["key_tail"].wait()
    squares_tail = tiles(
        WIDE, lambda i, cols, acc: gated(tail, cols, acc), jnp.zeros((K, 128), F32)
    )
    pl.semaphore_wait(barrier, n - 1 + m - 1)

    @pl.when(s < n - 1)
    def _():
        def start(i, cols, _):
            halo_copy(i, cols).start()
            return 0

        tiles(WIDE, start)

    loads["stream_head"].wait()
    loads["key_head"].wait()
    squares_head = tiles(
        WIDE, lambda i, cols, acc: gated(head, cols, acc), jnp.zeros((R - K, 128), F32)
    )
    squares = to_row(jnp.concatenate([squares_head, squares_tail], axis=0))
    row_send[0] = squares
    for d in range(1, m):
        row_copy(0, d).start()

    loads["rate"].wait()
    loads["gate_out"].wait()
    loads["cotangent"].wait()

    def recur(i, cols, _):
        value = gate_out[:, cols].astype(F32) * cotangent[:, cols].astype(F32)
        slow = rate[:, cols]
        row = lax.broadcasted_iota(jnp.int32, value.shape, 0)
        k = 1
        while k < R:
            factor = jnp.exp(-slow * k)
            if k < 8:
                moved = jnp.where(row < R - k, pltpu.roll(value, R - k, 0), 0.0)
            else:
                moved = jnp.concatenate([value[k:], jnp.zeros((k, value.shape[1]), F32)], axis=0)
            value = value + factor * moved
            k *= 2
        rev[:, cols] = value
        carry_send[:, cols] = value[0:1]
        return 0

    tiles(128, recur)

    def carry_copy(d):
        return copy(
            carry_send, carry_recv.at[d - 1], carry_sem, d - 1, (lax.rem(s + n - d, n), c)
        )

    def start_carry(d, _):
        carry_copy(d).start()
        return 0

    lax.fori_loop(1, s + 1, start_carry, 0)

    loads["fwd"].wait()
    loads["taps"].wait()

    def tap_spectrum(i, cols, _):
        fh[:, cols] = product2(fwd, slice(None), slice(0, K), taps_ref[:, cols])
        return 0

    tiles(WIDE, tap_spectrum)

    loads["residue"].wait()
    loads["query"].wait()

    def wait_carry(d, _):
        carry_copy(d).wait_recv()
        return 0

    lax.fori_loop(1, n - s, wait_carry, 0)
    block_decay = jnp.exp(-rate[...] * R)

    def horner(i, later):
        return block_decay * later + carry_recv[n - 2 - s - i]

    entering[...] = lax.fori_loop(0, n - 1 - s, horner, jnp.zeros((1, C), F32))

    def norm_factor(slow):
        z = 2.0 * slow
        poly = 1.0 - z / 6.0
        for k in (5.0, 4.0, 3.0, 2.0):
            poly = 1.0 - z / k * poly
        return jnp.sqrt(z * poly)

    def state(i, cols, _):
        slow = rate[:, cols]
        position = lax.broadcasted_iota(jnp.int32, (R, WIDE), 0).astype(F32)
        value = rev[:, cols] + jnp.exp(-slow * (R - position)) * entering[:, cols]
        rev[:, cols] = value
        gm[:, cols] = query[:, cols].astype(F32) * (residue[:, cols] * norm_factor(slow) * value)

        @pl.when((s > 0) & (lax.rem(c, 2) == 0))
        def _():
            gm_copy(i, cols).start()

        return 0

    tiles(WIDE, state)

    total = squares
    for d in range(1, m):
        row_copy(0, d).wait_recv()
        total = total + row_recv[0, d - 1]
    inv_row = lax.rsqrt(total / channel_total + EPSILON)
    row_send[2] = inv_row
    inv_col[...] = to_col(inv_row)

    @pl.when(s < n - 1)
    def _():
        inv_copy.start()

    def local_spectra(i, cols, _):
        gh[:, cols] = product2(fwd, slice(None), slice(0, R), gm[:, cols])
        value = raw[:, cols] * wide(inv_col[...])
        xh[:, cols] = product2(fwd, slice(None), slice(K, N), value)
        return 0

    tiles(WIDE, local_spectra)

    @pl.when(s > 0)
    def _():
        inv_copy.wait_recv()

    loads["lag"].wait()
    loads["inv"].wait()

    def at_line(d):
        return (lax.rem(a + d, A) * B + b, c)

    def rs_copy(i, d):
        return copy(
            gf.at[i, lax.rem(a + d, A)],
            rs_recv.at[i, d - 1],
            rs_sem,
            i * (A - 1) + d - 1,
            at_line(d),
        )

    def forward(i, cols, _):
        @pl.when(s > 0)
        def _():
            halo_copy(i, cols).wait_recv()
            halo = raw_halo[:, cols] * wide(to_col(inv_halo[...])[R - K :])
            xh[:, cols] = xh[:, cols] + product2(fwd, slice(None), slice(0, K), halo)

        xr, xi = xh[:H, cols], xh[H:, cols]
        gr, gi = gh[:H, cols], gh[H:, cols]
        spectrum = jnp.concatenate([gr * xr + gi * xi, gr * xi - gi * xr], axis=0)
        value = product2(lag, slice(None), slice(None), spectrum)
        for k in range(A):
            gf[i, k] = value[k * chunk : (k + 1) * chunk]

        def start(d, _):
            rs_copy(i, d).start()
            return 0

        lax.fori_loop(1, A, start, 0)

        fr, fi = fh[:H, cols], fh[H:, cols]
        spectrum = jnp.concatenate([fr * xr - fi * xi, fr * xi + fi * xr], axis=0)
        mixed = product2(inv, slice(K, N), slice(None), spectrum)
        factor = norm_factor(rate[:, cols])
        states = rev[:, cols]
        out_query[:, cols] = (mixed * (residue[:, cols] * factor * states)).astype(BF16)
        stored = (query[:, cols].astype(F32) * mixed).astype(BF16).astype(F32)
        res_all[s, :, cols] = factor * jnp.sum(stored * states, axis=0, keepdims=True)
        return 0

    tiles(WIDE, forward)

    @pl.when((s > 0) & (lax.rem(c, 2) == 1))
    def _():
        def start(i, cols, _):
            gm_copy(i, cols).start()
            return 0

        tiles(WIDE, start)

    def res_copy(d):
        return copy(res_all.at[s], res_all.at[s], res_sem, d - 1, (lax.rem(s + d, n), c))

    def start_res(d, _):
        res_copy(d).start()
        return 0

    lax.fori_loop(1, n, start_res, 0)

    def ex_copy(i):
        return copy(part.at[i], ex_recv.at[i], ex_sem, i, (a * B + (B - 1 - b), c))

    def ag_copy(i, d):
        return copy(ag.at[i, a], ag.at[i, a], ag_sem, i * (A - 1) + d - 1, at_line(d))

    def add_line(i, _):
        def add(d, total):
            rs_copy(i, d).wait_recv()
            return total + rs_recv[i, d - 1]

        part[i] = lax.fori_loop(1, A, add, gf[i, a])

        @pl.when(lax.rem(i, B) != b)
        def _():
            ex_copy(i).start()

        return 0

    lax.fori_loop(0, T, add_line, 0)
    scale = token_total**-0.5

    def fwd_copy(i):
        return copy(ag.at[i], ag.at[i], fwd_sem, i, (a * B + (B - 1 - b), c))

    def add_partner(i, _):
        @pl.when(lax.rem(i, B) == b)
        def _():
            total = part[i]
            if B == 2:
                ex_copy(i).wait_recv()
                total = total + ex_recv[i]
            ag[i, a] = total * scale

            def start(d, _):
                ag_copy(i, d).start()
                return 0

            lax.fori_loop(1, A, start, 0)

        return 0

    lax.fori_loop(0, T, add_partner, 0)

    def backward(i, cols, acc):
        @pl.when(s < n - 1)
        def _():
            gm_copy(i, cols).wait_recv()
            gh[:, cols] = gh[:, cols] + product2(fwd, slice(None), slice(R, N), gm_halo[:, cols])

        gr, gi = gh[:H, cols], gh[H:, cols]
        fr, fi = fh[:H, cols], fh[H:, cols]
        spectrum = jnp.concatenate([fr * gr + fi * gi, fr * gi - fi * gr], axis=0)
        grad = product2(inv, slice(0, R), slice(None), spectrum)
        value = gain[:, cols] * key[:, cols].astype(F32) * grad
        weighted[:, cols] = value
        return acc + lanes(value * stream[:, cols].astype(F32))

    dots = to_row(tiles(WIDE, backward, jnp.zeros((R, 128), F32)))
    row_send[1] = dots
    for d in range(1, m):
        row_copy(1, d).start()

    def gathered(i, _):
        @pl.when(lax.rem(i, B) == b)
        def _():
            def arrived(d, _):
                ag_copy(i, d).wait_recv()
                return 0

            lax.fori_loop(1, A, arrived, 0)
            if B == 2:
                fwd_copy(i).start()

        return 0

    lax.fori_loop(0, T, gathered, 0)
    for d in range(1, m):
        row_copy(1, d).wait_recv()
        dots = dots + row_recv[1, d - 1]
    dots_col = to_col(dots / channel_total)

    def finish(i, cols, _):
        scale_rows = wide(inv_col[...])
        pull = wide(inv_col[...] * inv_col[...] * dots_col)
        value = weighted[:, cols] - stream[:, cols].astype(F32) * pull
        out_stream[:, cols] = (scale_rows * value).astype(BF16)
        return 0

    tiles(WIDE, finish)

    def res_arrived(d, _):
        res_copy(d).wait_recv()
        return 0

    lax.fori_loop(1, n, res_arrived, 0)
    out_residue[...] = (
        lax.fori_loop(0, n, lambda i, total: total + res_all[i], jnp.zeros((1, C), F32)) * scale
    )

    def spread(i, cols, _):
        @pl.when(lax.rem(i, B) != b)
        def _():
            fwd_copy(i).wait_recv()

        for k in range(A):
            out_filter[k * chunk : (k + 1) * chunk, cols] = ag[i, k]
        return 0

    tiles(WIDE, spread)

    for d in range(1, m):
        row_copy(0, d).wait_send()
        row_copy(1, d).wait_send()

    def left(i, cols, _):
        @pl.when(s < n - 1)
        def _():
            halo_copy(i, cols).wait_send()

        @pl.when(s > 0)
        def _():
            gm_copy(i, cols).wait_send()

        def line(d, _):
            rs_copy(i, d).wait_send()
            return 0

        lax.fori_loop(1, A, line, 0)

        @pl.when(lax.rem(i, B) != b)
        def _():
            ex_copy(i).wait_send()

        @pl.when(lax.rem(i, B) == b)
        def _():
            def line(d, _):
                ag_copy(i, d).wait_send()
                return 0

            lax.fori_loop(1, A, line, 0)
            if B == 2:
                fwd_copy(i).wait_send()

        return 0

    tiles(WIDE, left)

    @pl.when(s < n - 1)
    def _():
        inv_copy.wait_send()

    def carry_sent(d, _):
        carry_copy(d).wait_send()
        return 0

    lax.fori_loop(1, s + 1, carry_sent, 0)

    def res_sent(d, _):
        res_copy(d).wait_send()
        return 0

    lax.fori_loop(1, n, res_sent, 0)


def hand_over(*refs):
    held, sem = refs[8:12], refs[12]
    into = [pltpu.make_async_copy(refs[i], held[i], sem.at[0, i]) for i in range(4)]
    away = [pltpu.make_async_copy(held[i], refs[4 + i], sem.at[1, i]) for i in range(4)]
    for one in into:
        one.start()
    for first, second in zip(into, away):
        first.wait()
        second.start()
    for one in away:
        one.wait()


def solution(mesh):
    n, m = mesh.shape["seq"], mesh.shape["chan"]

    def body(
        stream,
        norm_gain,
        gate_query,
        gate_key,
        gate_out,
        cotangent,
        medium_filter,
        long_residue,
        long_rate,
    ):
        R, C = stream.shape
        K = medium_filter.shape[0]
        N = R + K
        mats = [jnp.asarray(mat) for mat in transforms(R, K)]
        T = C // WIDE
        B = 2 if n % 2 == 0 else 1
        A = n // B
        vmem = pl.BlockSpec(memory_space=pltpu.VMEM)
        hbm = pl.BlockSpec(memory_space=pltpu.HBM)

        def buffer(*shape):
            return pltpu.VMEM(shape, F32)

        def sems(count):
            return pltpu.SemaphoreType.DMA((2, count))

        outs = pl.pallas_call(
            functools.partial(kernel, n, m),
            out_shape=(
                jax.ShapeDtypeStruct((R, C), BF16),
                jax.ShapeDtypeStruct((R, C), BF16),
                jax.ShapeDtypeStruct((K, C), F32),
                jax.ShapeDtypeStruct((1, C), F32),
            ),
            in_specs=[hbm] * 12,
            out_specs=(vmem,) * 4,
            scratch_shapes=[
                pltpu.VMEM((R, C), BF16),
                buffer(1, C),
                pltpu.VMEM((R, C), BF16),
                pltpu.VMEM((R, C), BF16),
                pltpu.VMEM((R, C), BF16),
                pltpu.VMEM((R, C), BF16),
                buffer(K, C),
                buffer(1, C),
                buffer(1, C),
                *(pltpu.VMEM(mat.shape, BF16) for mat in mats),
                buffer(R, C),
                buffer(1, C),
                buffer(R, C),
                buffer(R, C),
                buffer(K, C),
                buffer(K, C),
                buffer(R, 128),
                buffer(3, 8, R),
                buffer(2, m - 1, 8, R),
                buffer(8, R),
                buffer(1, C),
                buffer(n - 1, 1, C),
                buffer(N, C),
                buffer(N, C),
                buffer(N, C),
                buffer(T, A, K // A, WIDE),
                buffer(T, A - 1, K // A, WIDE),
                buffer(T, K // A, WIDE),
                buffer(T, K // A, WIDE),
                buffer(T, A, K // A, WIDE),
                buffer(n, 1, C),
                buffer(R, C),
                pltpu.SemaphoreType.DMA((14,)),
                sems(1),
                sems(T),
                sems(T),
                sems(2 * (m - 1)),
                sems(n - 1),
                sems(T * (A - 1)),
                sems(T),
                sems(T * (A - 1)),
                sems(T),
                sems(n - 1),
            ],
            compiler_params=pltpu.CompilerParams(
                collective_id=0, has_side_effects=True, vmem_limit_bytes=62 * 2**20
            ),
            cost_estimate=pl.CostEstimate(
                flops=2 * (2 * N + 2 * R + 2 * K) * N * C * 2,
                bytes_accessed=8 * R * C * 2,
                transcendentals=R * C,
            ),
        )(
            stream,
            norm_gain[None],
            gate_query,
            gate_key,
            gate_out,
            cotangent,
            medium_filter,
            long_residue[None],
            long_rate[None],
            *mats,
        )
        outs = pl.pallas_call(
            hand_over,
            out_shape=tuple(jax.ShapeDtypeStruct(out.shape, out.dtype) for out in outs),
            in_specs=[hbm] * 4,
            out_specs=(hbm,) * 4,
            scratch_shapes=[
                *(pltpu.VMEM(out.shape, out.dtype) for out in outs),
                pltpu.SemaphoreType.DMA((2, 4)),
            ],
            compiler_params=pltpu.CompilerParams(vmem_limit_bytes=62 * 2**20),
        )(*outs)
        return outs[0], outs[1], outs[2], outs[3][0]

    in_specs = (
        P("seq", "chan"),
        P("chan"),
        P("seq", "chan"),
        P("seq", "chan"),
        P("seq", "chan"),
        P("seq", "chan"),
        P(None, "chan"),
        P("chan"),
        P("chan"),
    )
    out_specs = (P("seq", "chan"), P("seq", "chan"), P(None, "chan"), P("chan"))
    return jax.shard_map(body, mesh=mesh, in_specs=in_specs, out_specs=out_specs, check_vma=False)
```
